256 devices in a mesh: fsdp: 32 (over y, z), rep: 8 (over x, core).
Axes of the slice: x: 4, y: 4, z: 8, core: 2. Of those that a mesh axis runs over, the one named last changes fastest.
Arguments:
- gradient: float32 [8, 4096, 6656], P('rep', 'fsdp')
- second_moment: float32 [4096, 6656], P('fsdp'), may hold values from 0.0001 to 0.1
- owner_cols: int32 [8, 1, 32], replicated, may hold values from -1 to 12, as said below
- stat_left: float32 [32, 1, 8, 512, 512], P('fsdp', None, None, 'rep'), as said below
- stat_right: float32 [32, 1, 8, 512, 512], P('fsdp', None, None, 'rep'), as said below
- root_left: float32 [32, 1, 8, 512, 512], P('fsdp', None, None, 'rep'), as said below
- root_right: float32 [32, 1, 8, 512, 512], P('fsdp', None, None, 'rep'), as said below
Outputs:
- direction: float32 [4096, 6656], P('fsdp')
- moment_new: float32 [4096, 6656], P('fsdp')
- left_new: float32 [32, 1, 8, 512, 512], P('fsdp', None, None, 'rep')
- right_new: float32 [32, 1, 8, 512, 512], P('fsdp', None, None, 'rep')
The draws below stay inside these ranges and needn't reach their ends.
Inputs may be any that keep to these rules, and one draw needn't show every extreme that they name: owner_cols[b, k, o] is the column block of block row b kept in slot k of owner o, or -1 for an empty slot; every column block of every block row is kept in exactly one slot. `stat_left`: each block is symmetric. `stat_right`: each block is symmetric. `root_left`: each block is symmetric. `root_right`: each block is symmetric.
All inputs are finite; a program needn't handle non-finite values.
Results may differ from the reference program's by a relative error of at most 0.000071.
Values sent between devices are 32-bit elements; how exact they have to be, the bound alone decides.
No kernel may reach another device: no remote copies, remote signals or barrier semaphores. Data moves between devices by JAX's collectives and lax.ppermute only.
A program may use at most 128 MiB of HBM per device.

```python
import math
import jax
import jax.numpy as jnp
from jax import lax

D = 6656
BLOCK = 512
ROWS = 4096
COL_BLOCKS = 13
ROW_BLOCKS = 8
SLOTS = 1
N_FSDP = 32
N_REP = 8


def symmetrize(off_part, diagonal, spread):
    side = off_part.shape[-1]
    mirror = (off_part + jnp.swapaxes(off_part, -1, -2)) * (spread / math.sqrt(2.0 * side))
    eye_mask = jnp.arange(side)[:, None] == jnp.arange(side)[None, :]
    return mirror + jnp.where(eye_mask, diagonal[..., :, None], 0.0)


def symmetric_draw(key, spread, diag_lo, diag_hi):
    full_shape = (N_FSDP, SLOTS, ROW_BLOCKS, BLOCK, BLOCK)
    key_off, key_diag = jax.random.split(key)
    off_part = jax.random.normal(key_off, full_shape, jnp.float32)
    diagonal = jnp.exp(jax.random.uniform(key_diag, full_shape[:-1], jnp.float32, math.log(diag_lo), math.log(diag_hi)))
    return symmetrize(off_part, diagonal, spread)


def draw_stat_left(key, part):
    key = jax.random.fold_in(key, 21)
    return symmetric_draw(key, 1.0, 0.5, 4.0)


def draw_stat_right(key, part):
    key = jax.random.fold_in(key, 22)
    return symmetric_draw(key, 1.0, 0.5, 4.0)


def draw_root_left(key, part):
    key = jax.random.fold_in(key, 23)
    return symmetric_draw(key, 0.5, 1.0, 2.0)


def draw_root_right(key, part):
    key = jax.random.fold_in(key, 24)
    return symmetric_draw(key, 0.5, 1.0, 2.0)


def draw_gradient(key, part):
    key = jax.random.fold_in(key, 31)
    key_noise, key_row, key_col = jax.random.split(key, 3)
    row_pos = (jnp.arange(ROWS, dtype=jnp.int32) % BLOCK).astype(jnp.float32)
    jitter = jax.random.uniform(key_row, (ROWS,), jnp.float32)
    row_scale = jnp.exp(math.log(10.0) * (row_pos + jitter) / BLOCK)
    col_scale = jnp.exp(jax.random.uniform(key_col, (D,), jnp.float32, 0.0, math.log(10.0)))
    values = 0.01 * jax.random.normal(key_noise, (N_REP, ROWS, D), jnp.float32)
    return values * row_scale[None, :, None] * col_scale[None, None, :]


def draw_owner_cols(key, part):
    key = jax.random.fold_in(key, 11)
    subkeys = jax.random.split(key, ROW_BLOCKS)

    def one_row(subkey):
        shuffled = jax.random.permutation(subkey, SLOTS * N_FSDP)
        position = jnp.argsort(shuffled).astype(jnp.int32)
        return jnp.where(position < COL_BLOCKS, position, -1).astype(jnp.int32).reshape(SLOTS, N_FSDP)
    return jax.vmap(one_row)(subkeys)


def shard_levels(own_key, shape, pieces, low, top_value):
    factor_of, own = 1.0, jax.random.fold_in(own_key, 6)
    for dim, shards_of in pieces:
        heights = jnp.exp(jax.random.uniform(jax.random.fold_in(own, dim), (shards_of,), jnp.float32, low / len(pieces), top_value / len(pieces)))
        factor_of = factor_of * jnp.repeat(heights, shape[dim] // shards_of).reshape([-1 if axis == dim else 1 for axis in range(len(shape))])
    return factor_of


def setup_inputs(seed: int = 0) -> dict:
    keys = jax.random.split(jax.random.key(seed), 8)
    return {
        "gradient": draw_gradient(jax.random.fold_in(keys[7], 71), 0),
        "second_moment": jnp.clip(jnp.exp(math.log(0.1) - 6.9077553 * jax.random.uniform(keys[1], (ROWS, D), jnp.float32) ** shard_levels(keys[1], (ROWS, D), ((0, 32),), -0.2, 0.2)), 0.0001, 0.1),
        "owner_cols": draw_owner_cols(jax.random.fold_in(keys[7], 71), 0),
        "stat_left": draw_stat_left(jax.random.fold_in(keys[7], 71), 0),
        "stat_right": draw_stat_right(jax.random.fold_in(keys[7], 71), 0),
        "root_left": draw_root_left(jax.random.fold_in(keys[7], 71), 0),
        "root_right": draw_root_right(jax.random.fold_in(keys[7], 71), 0),
    }


SHAMPOO_DECAY = 0.9
ADAM_DECAY = 0.95
ADAM_EPS = 1e-08
NORM_EPS = 1e-06
HIGHEST = lax.Precision.HIGHEST

def reference(gradient, second_moment, owner_cols, stat_left, stat_right, root_left, root_right):
    averaged = lax.optimization_barrier(jnp.sum(gradient, axis=0)) / N_REP
    moment_new = ADAM_DECAY * second_moment + (1.0 - ADAM_DECAY) * averaged * averaged
    adam_step = averaged / (jnp.sqrt(moment_new) + ADAM_EPS)
    blocks = averaged.reshape(ROW_BLOCKS, BLOCK, COL_BLOCKS, BLOCK).transpose(0, 2, 1, 3)
    gram_left = jnp.einsum('bcij,bclj->bcil', blocks, blocks, precision=HIGHEST)
    gram_right = jnp.einsum('bcji,bcjl->bcil', blocks, blocks, precision=HIGHEST)
    slot_cols = jnp.transpose(owner_cols, (2, 1, 0))
    held_mask = (slot_cols >= 0)[..., None, None]
    row_index = jnp.arange(ROW_BLOCKS, dtype=jnp.int32)[None, None, :] + jnp.zeros_like(slot_cols)
    col_index = jnp.maximum(slot_cols, 0).astype(jnp.int32)
    left_new = SHAMPOO_DECAY * stat_left + (1.0 - SHAMPOO_DECAY) * jnp.where(held_mask, gram_left[row_index, col_index], 0.0)
    right_new = SHAMPOO_DECAY * stat_right + (1.0 - SHAMPOO_DECAY) * jnp.where(held_mask, gram_right[row_index, col_index], 0.0)
    matches = owner_cols[:, None, :, :] == jnp.arange(COL_BLOCKS, dtype=jnp.int32)[None, :, None, None]
    flat_slot = jnp.argmax(matches.reshape(ROW_BLOCKS, COL_BLOCKS, SLOTS * N_FSDP), axis=2).astype(jnp.int32)
    slot_k = flat_slot // N_FSDP
    slot_o = flat_slot % N_FSDP
    block_row = jnp.arange(ROW_BLOCKS, dtype=jnp.int32)[:, None] + jnp.zeros_like(flat_slot)
    left_roots = root_left[slot_o, slot_k, block_row]
    right_roots = root_right[slot_o, slot_k, block_row]
    left_applied = jnp.einsum('bcij,bcjl->bcil', left_roots, blocks, precision=HIGHEST)
    applied = jnp.einsum('bcij,bcjl->bcil', left_applied, right_roots, precision=HIGHEST)
    adam_norm = jnp.sqrt(lax.optimization_barrier(jnp.sum(jnp.square(adam_step).reshape(ROW_BLOCKS, BLOCK, COL_BLOCKS, BLOCK), axis=(1, 3))))
    shampoo_norm = jnp.sqrt(lax.optimization_barrier(jnp.sum(jnp.square(applied), axis=(2, 3))))
    grafted = applied * (adam_norm / (shampoo_norm + NORM_EPS))[:, :, None, None]
    direction = grafted.transpose(0, 2, 1, 3).reshape(ROWS, D)
    return (direction, moment_new, left_new, right_new)
```

```python
import functools

import jax
import jax.numpy as jnp
from jax import lax
from jax.experimental import pallas as pl
from jax.experimental.pallas import tpu as pltpu
from jax.sharding import PartitionSpec as P

SHAMPOO_DECAY = 0.9
ADAM_DECAY = 0.95
ADAM_EPS = 1e-08
NORM_EPS = 1e-06
PARAMS = pltpu.CompilerParams(vmem_limit_bytes=32 * 1024 * 1024)
F32 = jnp.float32
BF16 = jnp.bfloat16


def rep_shift(value, step, count):
    return lax.ppermute(value, "rep", [(i, (i + step) % count) for i in range(count)])


def pick(array, index, axis=0):
    return lax.dynamic_index_in_dim(array, index, axis, keepdims=False)


def split(value):
    high = value.astype(BF16)
    return high, (value - high.astype(F32)).astype(BF16)


def dot3(a, b, dims):
    dot = functools.partial(
        lax.dot_general, dimension_numbers=(dims, ((), ())), preferred_element_type=F32
    )
    return dot(a[0], b[0]) + (dot(a[0], b[1]) + dot(a[1], b[0]))


def moment_kernel(cols, replicas, ids, owner_cols, *refs):
    parts, second = refs[:4], refs[4]
    moment, squares, packed, averaged = refs[5:]
    row = ids[1]
    width = packed.shape[-1]
    squares[...] = jnp.zeros_like(squares)
    for c in range(cols):
        here = slice(c * width, (c + 1) * width)
        summed = (parts[0][:, here] + parts[1][:, here]) + (parts[2][:, here] + parts[3][:, here])
        mean = summed / replicas
        averaged[:, here] = mean
        new = ADAM_DECAY * second[:, here] + (1.0 - ADAM_DECAY) * mean * mean
        moment[:, here] = new
        step = mean / (jnp.sqrt(new) + ADAM_EPS)
        square = jnp.sum(step * step, axis=0, keepdims=True)
        lanes = square[:, 0:128]
        for k in range(1, width // 128):
            lanes = lanes + square[:, k * 128 : (k + 1) * 128]
        lane = (c // 8) * 128
        squares[c % 8 : c % 8 + 1, lane : lane + 128] = lanes
    for o in range(packed.shape[0]):
        col = owner_cols[row, o]
        start = pl.multiple_of(jnp.maximum(col, 0) * width, width)
        piece = averaged[:, pl.ds(start, width)]
        packed[o] = jnp.where(col >= 0, piece, 0.0)


def load_block(blocks, high, low):
    pieces, quarters, rows, _ = blocks.shape
    for i in range(quarters):
        for r in range(pieces):
            at = (i * pieces + r) * rows
            high[at : at + rows, :], low[at : at + rows, :] = split(blocks[r, i])


def apply_kernel(ids, blocks, *refs):
    roots = refs[:8]
    applied, gh, gl, lh, ll, rh, rl, whole = refs[8:]
    count, side = 8, whole.shape[0]
    share = side // count
    load_block(blocks, gh, gl)
    for k in range(count):
        start = pl.multiple_of(lax.rem(ids[0] - k + count, count) * share, share)
        lh[pl.ds(start, share), :], ll[pl.ds(start, share), :] = split(roots[k][0])
        rh[pl.ds(start, share), :], rl[pl.ds(start, share), :] = split(roots[k][1])
    right = dot3((gh[...], gl[...]), (rh[...], rl[...]), ((1,), (0,)))
    value = dot3((lh[...], ll[...]), split(right), ((1,), (0,)))
    whole[...] = value
    norm = jnp.sqrt(jnp.sum(value * value, keepdims=True))
    scale = 1.0 / (norm + NORM_EPS)
    pieces, quarters, rows, _ = applied.shape
    for i in range(quarters):
        for r in range(pieces):
            at = (i * pieces + r) * rows
            applied[r, i] = whole[at : at + rows, :] * scale


def gram_kernel(ids, blocks, squares, *refs):
    outs = refs[:8]
    gh, gl, left, right = refs[8:]
    count, side = 8, left.shape[0]
    share = side // count
    load_block(blocks, gh, gl)
    g = (gh[...], gl[...])
    left[...] = dot3(g, g, ((1,), (1,)))
    right[...] = dot3(g, g, ((0,), (0,)))
    for k in range(count):
        start = pl.multiple_of(lax.rem(ids[0] + k, count) * share, share)
        outs[k][0:share, :] = left[pl.ds(start, share), :]
        outs[k][share : 2 * share, :] = right[pl.ds(start, share), :]
        outs[k][2 * share :, :] = squares[...]


def stat_kernel(ids, moment, stat_left, stat_right, *refs):
    grams = refs[:8]
    moment_new, left, right = refs[8:]
    moment_new[...] = moment[...]
    share = left.shape[1]
    for k in range(8):
        b = lax.rem(ids[0] - k + 8, 8)
        left[b] = SHAMPOO_DECAY * stat_left[b] + (1.0 - SHAMPOO_DECAY) * grams[k][0:share, :]
        right[b] = (
            SHAMPOO_DECAY * stat_right[b] + (1.0 - SHAMPOO_DECAY) * grams[k][share : 2 * share, :]
        )


def direction_kernel(ids, owner_cols, returned, *refs):
    grams = refs[:8]
    direction, norms = refs[8:]
    tail = grams[0].shape[0] - 8
    row = ids[1]
    width = returned.shape[-1]
    total = grams[0][tail:, :]
    for k in range(1, 8):
        total = total + grams[k][tail:, :]
    for c in range(direction.shape[-1] // width):
        lane = (c // 8) * 128
        lanes = total[c % 8 : c % 8 + 1, lane : lane + 128]
        norm = jnp.sqrt(jnp.sum(lanes, axis=1, keepdims=True))
        norms[c : c + 1, :] = jnp.broadcast_to(norm, (1, 128))
    for o in range(returned.shape[0]):
        col = owner_cols[row, o]

        @pl.when(col >= 0)
        def _():
            norm = norms[pl.ds(col, 1), :][:, 0:1]
            start = pl.multiple_of(col * width, width)
            direction[:, pl.ds(start, width)] = returned[o] * norm


def root_kernel(ids, root_left, root_right, *outs):
    for k in range(8):
        to = lax.rem(ids[0] + k, 8)
        outs[k][0] = root_left[to]
        outs[k][1] = root_right[to]


def staged(kernel, n_small, n_in, n_out, *refs):
    cut = [n_small, n_in, n_out, n_in, n_out]
    groups, at = [], 0
    for size in cut:
        groups.append(refs[at : at + size])
        at += size
    small, sources, targets, ins, outs = groups
    in_sems, out_sems = refs[at : at + 2]
    loads = [
        pltpu.make_async_copy(src, dst, in_sems.at[i])
        for i, (src, dst) in enumerate(zip(sources, ins))
    ]
    for load in loads:
        load.start()
    for load in loads:
        load.wait()
    kernel(*small, *ins, *outs, *refs[at + 2 :])
    stores = [
        pltpu.make_async_copy(src, dst, out_sems.at[i])
        for i, (src, dst) in enumerate(zip(outs, targets))
    ]
    for store in stores:
        store.start()
    for store in stores:
        store.wait()


def call(kernel, outs, small, ins, scratch):
    hbm = pl.BlockSpec(memory_space=pltpu.HBM)
    smem = pl.BlockSpec(memory_space=pltpu.SMEM)
    held = [pltpu.VMEM(x.shape, F32) for x in ins] + [pltpu.VMEM(s, F32) for s in outs]
    sems = [pltpu.SemaphoreType.DMA((len(ins),)), pltpu.SemaphoreType.DMA((len(outs),))]
    return pl.pallas_call(
        functools.partial(staged, kernel, len(small), len(ins), len(outs)),
        out_shape=[pltpu.HBM(shape, F32) for shape in outs],
        in_specs=[smem] * len(small) + [hbm] * len(ins),
        out_specs=[hbm] * len(outs),
        scratch_shapes=held + sems + scratch,
        compiler_params=PARAMS,
    )(*small, *[pltpu.with_memory_space_constraint(x, pltpu.HBM) for x in ins])


def shards(gradient, second_moment, owner_cols, stat_left, stat_right, root_left, root_right):
    shard_rows, full_width = gradient.shape[1:]
    side = stat_left.shape[-1]
    owners = lax.axis_size("fsdp")
    reps = lax.axis_size("rep")
    chips = reps // 2
    cols = full_width // side
    rows = shard_rows // reps
    share = side // reps
    quarters = side // shard_rows
    block_rows = owner_cols.shape[0]
    rep = lax.axis_index("rep")
    chip, core = rep // 2, rep % 2
    my_row = lax.axis_index("fsdp") // quarters
    ids = jnp.stack([rep, my_row]).astype(jnp.int32)
    oc = owner_cols[:, 0, :]
    barrier = lax.optimization_barrier

    grad = gradient[0].reshape(chips, 2, rows, full_width)
    swap = [(i, i ^ 1) for i in range(reps)]
    pieces = {}
    for k in (2, 1, 3, 0):
        here = pick(grad, (chip + k) % chips)
        other = lax.ppermute(pick(here, 1 - core), "rep", swap)
        pieces[k] = pick(here, core) + other
    parts = [pieces[0]] + [rep_shift(pieces[k], 2 * k, reps) for k in (1, 2, 3)]
    second = lax.dynamic_slice_in_dim(second_moment, rep * rows, rows, 0)
    later_ids, _ = barrier((ids, pieces[0]))
    stats = (block_rows, share, side)
    pair = (2, share, side)
    roots = call(root_kernel, [pair] * reps, [later_ids], [root_left[0, 0], root_right[0, 0]], [])

    strip = (rows, full_width)
    tail = (8, side)
    moment, squares, packed = call(
        functools.partial(moment_kernel, cols, reps),
        [strip, tail, (owners, rows, side)],
        [ids, oc],
        [*parts, second],
        [pltpu.VMEM(strip, F32)],
    )
    packed, *roots = barrier((packed, *roots))
    arrived = lax.all_to_all(packed, "fsdp", 0, 0, tiled=True)
    moment_all = lax.all_gather(moment, "rep", axis=0, tiled=True)
    roots = [r if k == 0 else rep_shift(r, k, reps) for k, r in enumerate(roots)]
    arrived, squares, *roots = barrier((arrived, squares, *roots))

    square_sum = squares
    for bits in (1, 2, 3):
        square_sum = square_sum + lax.ppermute(
            squares, "fsdp", [(i, i ^ bits) for i in range(owners)]
        )
    blocks = lax.all_to_all(
        arrived.reshape(block_rows, quarters, rows, side), "rep", 0, 0, tiled=True
    )
    half = pltpu.VMEM((side, side), BF16)
    full = pltpu.VMEM((side, side), F32)
    (applied,) = call(
        apply_kernel, [blocks.shape], [ids], [blocks, *roots], [half] * 6 + [full]
    )
    spread = lax.all_to_all(applied, "rep", 0, 0, tiled=True)
    grams = call(
        gram_kernel,
        [(2 * share + 8, side)] * reps,
        [ids],
        [blocks, square_sum],
        [half] * 2 + [full] * 2,
    )
    spread, *grams = barrier((spread, *grams))
    returned = lax.all_to_all(spread.reshape(owners, rows, side), "fsdp", 0, 0, tiled=True)
    grams = [g if k == 0 else rep_shift(g, k, reps) for k, g in enumerate(grams)]
    returned, *grams = barrier((returned, *grams))
    (part,) = call(
        direction_kernel,
        [strip],
        [ids, oc],
        [returned, *grams],
        [pltpu.VMEM((16, 128), F32)],
    )
    direction = lax.all_gather(part, "rep", axis=0, tiled=True)
    moment_new, left_new, right_new = call(
        stat_kernel,
        [(shard_rows, full_width), stats, stats],
        [ids],
        [moment_all, stat_left[0, 0], stat_right[0, 0], *grams],
        [],
    )
    return (direction, moment_new, left_new[None, None], right_new[None, None])


def solution(mesh):
    return jax.shard_map(
        shards,
        mesh=mesh,
        in_specs=(
            P("rep", "fsdp", None),
            P("fsdp", None),
            P(),
            P("fsdp", None, None, "rep", None),
            P("fsdp", None, None, "rep", None),
            P("fsdp", None, None, "rep", None),
            P("fsdp", None, None, "rep", None),
        ),
        out_specs=(
            P("fsdp", None),
            P("fsdp", None),
            P("fsdp", None, None, "rep", None),
            P("fsdp", None, None, "rep", None),
        ),
        check_vma=False,
    )
```

```python
import functools

import jax
import jax.numpy as jnp
from jax import lax
from jax.experimental import pallas as pl
from jax.experimental.pallas import tpu as pltpu
from jax.sharding import PartitionSpec as P

SHAMPOO_DECAY = 0.9
ADAM_DECAY = 0.95
ADAM_EPS = 1e-08
NORM_EPS = 1e-06
PARAMS = pltpu.CompilerParams(vmem_limit_bytes=32 * 1024 * 1024)
F32 = jnp.float32
BF16 = jnp.bfloat16


def rep_shift(value, step, count):
    return lax.ppermute(value, "rep", [(i, (i + step) % count) for i in range(count)])


def pick(array, index, axis=0):
    return lax.dynamic_index_in_dim(array, index, axis, keepdims=False)


def split(value):
    high = value.astype(BF16)
    return high, (value - high.astype(F32)).astype(BF16)


def dot3(a, b, dims):
    dot = functools.partial(
        lax.dot_general, dimension_numbers=(dims, ((), ())), preferred_element_type=F32
    )
    return dot(a[0], b[0]) + (dot(a[0], b[1]) + dot(a[1], b[0]))


def moment_kernel(cols, replicas, ids, owner_cols, *refs):
    parts, second = refs[:4], refs[4]
    moment, squares, packed, averaged = refs[5:]
    row = ids[1]
    width = packed.shape[-1]
    squares[...] = jnp.zeros_like(squares)
    for c in range(cols):
        here = slice(c * width, (c + 1) * width)
        summed = (parts[0][:, here] + parts[1][:, here]) + (parts[2][:, here] + parts[3][:, here])
        mean = summed / replicas
        averaged[:, here] = mean
        new = ADAM_DECAY * second[:, here] + (1.0 - ADAM_DECAY) * mean * mean
        moment[:, here] = new
        step = mean / (jnp.sqrt(new) + ADAM_EPS)
        square = jnp.sum(step * step, axis=0, keepdims=True)
        lanes = square[:, 0:128]
        for k in range(1, width // 128):
            lanes = lanes + square[:, k * 128 : (k + 1) * 128]
        lane = (c // 8) * 128
        squares[c % 8 : c % 8 + 1, lane : lane + 128] = lanes
    for o in range(packed.shape[0]):
        col = owner_cols[row, o]
        start = pl.multiple_of(jnp.maximum(col, 0) * width, width)
        piece = averaged[:, pl.ds(start, width)]
        packed[o] = jnp.where(col >= 0, piece, 0.0)


def load_block(blocks, high, low):
    pieces, quarters, rows, _ = blocks.shape
    for i in range(quarters):
        for r in range(pieces):
            at = (i * pieces + r) * rows
            high[at : at + rows, :], low[at : at + rows, :] = split(blocks[r, i])


def apply_kernel(ids, blocks, *refs):
    roots = refs[:8]
    applied, gh, gl, left, right, whole = refs[8:]
    count, side = 8, whole.shape[0]
    share = side // count
    part = side // 4
    load_block(blocks, gh, gl)
    for k in range(count):
        other = lax.rem(ids[0] - k + count, count)
        start = pl.multiple_of(other * share, share)
        for j in range(3):
            lane = pl.multiple_of(lax.rem(other // 2 + j, 4) * part, part)
            here = slice(j * part, (j + 1) * part)
            left[pl.ds(start, share), pl.ds(lane, part)] = roots[k][0, :, here]
            right[pl.ds(start, share), pl.ds(lane, part)] = roots[k][1, :, here]
    for x in range(4):
        before = (x + 3) % 4
        at, to = slice(x * part, (x + 1) * part), slice(before * part, (before + 1) * part)
        left[at, to] = left[to, at].T
        right[at, to] = right[to, at].T
    product = dot3((gh[...], gl[...]), split(right[...]), ((1,), (0,)))
    value = dot3(split(left[...]), split(product), ((1,), (0,)))
    whole[...] = value
    norm = jnp.sqrt(jnp.sum(value * value, keepdims=True))
    scale = 1.0 / (norm + NORM_EPS)
    pieces, quarters, rows, _ = applied.shape
    for i in range(quarters):
        for r in range(pieces):
            at = (i * pieces + r) * rows
            applied[r, i] = whole[at : at + rows, :] * scale


def gram_kernel(ids, blocks, squares, *refs):
    outs = refs[:8]
    gh, gl, left, right = refs[8:]
    count, side = 8, left.shape[0]
    share = side // count
    load_block(blocks, gh, gl)
    g = (gh[...], gl[...])
    left[...] = dot3(g, g, ((1,), (1,)))
    right[...] = dot3(g, g, ((0,), (0,)))
    for k in range(count):
        start = pl.multiple_of(lax.rem(ids[0] + k, count) * share, share)
        outs[k][0:share, :] = left[pl.ds(start, share), :]
        outs[k][share : 2 * share, :] = right[pl.ds(start, share), :]
        outs[k][2 * share :, :] = squares[...]


def stat_kernel(ids, own, swapped, stat_left, stat_right, *refs):
    grams = refs[:8]
    moment_new, left, right = refs[8:]
    core = lax.rem(ids[0], 2)
    rows = own.shape[0] // 4
    for x in range(4):
        here = slice(x * rows, (x + 1) * rows)
        at = pl.multiple_of((2 * x + core) * rows, rows)
        moment_new[pl.ds(at, rows), :] = own[here, :]
        at = pl.multiple_of((2 * x + 1 - core) * rows, rows)
        moment_new[pl.ds(at, rows), :] = swapped[here, :]
    share = left.shape[1]
    for k in range(8):
        b = lax.rem(ids[0] - k + 8, 8)
        left[b] = SHAMPOO_DECAY * stat_left[b] + (1.0 - SHAMPOO_DECAY) * grams[k][0:share, :]
        right[b] = (
            SHAMPOO_DECAY * stat_right[b] + (1.0 - SHAMPOO_DECAY) * grams[k][share : 2 * share, :]
        )


def direction_kernel(ids, owner_cols, returned, *refs):
    grams = refs[:8]
    low, high, direction, norms = refs[8:]
    tail = grams[0].shape[0] - 8
    row = ids[1]
    width = returned.shape[-1]
    total = grams[0][tail:, :]
    for k in range(1, 8):
        total = total + grams[k][tail:, :]
    for c in range(direction.shape[-1] // width):
        lane = (c // 8) * 128
        lanes = total[c % 8 : c % 8 + 1, lane : lane + 128]
        norm = jnp.sqrt(jnp.sum(lanes, axis=1, keepdims=True))
        norms[c : c + 1, :] = jnp.broadcast_to(norm, (1, 128))
    for o in range(returned.shape[0]):
        col = owner_cols[row, o]

        @pl.when(col >= 0)
        def _():
            norm = norms[pl.ds(col, 1), :][:, 0:1]
            start = pl.multiple_of(col * width, width)
            direction[:, pl.ds(start, width)] = returned[o] * norm

    middle = low.shape[1]
    low[...] = direction[:, :middle]
    high[...] = direction[:, middle:]


def staged(kernel, n_small, n_in, n_out, *refs):
    cut = [n_small, n_in, n_out, n_in, n_out]
    groups, at = [], 0
    for size in cut:
        groups.append(refs[at : at + size])
        at += size
    small, sources, targets, ins, outs = groups
    in_sems, out_sems = refs[at : at + 2]
    loads = [
        pltpu.make_async_copy(src, dst, in_sems.at[i])
        for i, (src, dst) in enumerate(zip(sources, ins))
    ]
    for load in loads:
        load.start()
    for load in loads:
        load.wait()
    kernel(*small, *ins, *outs, *refs[at + 2 :])
    stores = [
        pltpu.make_async_copy(src, dst, out_sems.at[i])
        for i, (src, dst) in enumerate(zip(outs, targets))
    ]
    for store in stores:
        store.start()
    for store in stores:
        store.wait()


def call(kernel, outs, small, ins, scratch):
    hbm = pl.BlockSpec(memory_space=pltpu.HBM)
    smem = pl.BlockSpec(memory_space=pltpu.SMEM)
    held = [pltpu.VMEM(x.shape, F32) for x in ins] + [pltpu.VMEM(s, F32) for s in outs]
    sems = [pltpu.SemaphoreType.DMA((len(ins),)), pltpu.SemaphoreType.DMA((len(outs),))]
    return pl.pallas_call(
        functools.partial(staged, kernel, len(small), len(ins), len(outs)),
        out_shape=[pltpu.HBM(shape, F32) for shape in outs],
        in_specs=[smem] * len(small) + [hbm] * len(ins),
        out_specs=[hbm] * len(outs),
        scratch_shapes=held + sems + scratch,
        compiler_params=PARAMS,
    )(*small, *[pltpu.with_memory_space_constraint(x, pltpu.HBM) for x in ins])


def root_plan(ids, ins, outs):
    chip = ids[0] // 2
    for k, out in enumerate(outs):
        to = lax.rem(ids[0] + k, 8)
        for side in range(2):
            for j in range(3):
                lane = pl.multiple_of(lax.rem(chip + j, 4) * 128, 128)
                yield (
                    ins[side].at[to, :, pl.ds(lane, 128)],
                    out.at[side, :, slice(j * 128, (j + 1) * 128)],
                )


def place_plan(ids, ins, outs):
    chip, core = ids[0] // 2, ids[0] % 2
    rows, middle = ins[0].shape
    for j, piece in enumerate(ins):
        owner = core if j < 8 else 1 - core
        from_chip = lax.rem(chip + (0, 3, 1, 2)[j % 8 // 2], 4)
        start = pl.multiple_of((from_chip * 2 + owner) * rows, rows)
        columns = slice(j % 2 * middle, (j % 2 + 1) * middle)
        yield piece, outs[0].at[pl.ds(start, rows), columns]


def copying(plan, n_small, n_in, n_out, *refs):
    small, ins = refs[:n_small], refs[n_small : n_small + n_in]
    outs = refs[n_small + n_in : n_small + n_in + n_out]
    held, (sems, out_sems) = refs[n_small + n_in + n_out : -2], refs[-2:]
    loads = [
        pltpu.make_async_copy(src, dst, sems.at[i])
        for i, (src, dst) in enumerate(plan(*small, ins, held))
    ]
    stores = [
        pltpu.make_async_copy(src, dst, out_sems.at[i])
        for i, (src, dst) in enumerate(zip(held, outs))
    ]
    for copies in (loads, stores):
        for copy in copies:
            copy.start()
        for copy in copies:
            copy.wait()


def shuffle(plan, outs, small, ins, count):
    hbm = pl.BlockSpec(memory_space=pltpu.HBM)
    smem = pl.BlockSpec(memory_space=pltpu.SMEM)
    return pl.pallas_call(
        functools.partial(copying, plan, len(small), len(ins), len(outs)),
        out_shape=[pltpu.HBM(shape, F32) for shape in outs],
        in_specs=[smem] * len(small) + [hbm] * len(ins),
        out_specs=[hbm] * len(outs),
        scratch_shapes=[pltpu.VMEM(shape, F32) for shape in outs]
        + [pltpu.SemaphoreType.DMA((count,)), pltpu.SemaphoreType.DMA((len(outs),))],
        compiler_params=PARAMS,
    )(*small, *[pltpu.with_memory_space_constraint(x, pltpu.HBM) for x in ins])


def shards(gradient, second_moment, owner_cols, stat_left, stat_right, root_left, root_right):
    shard_rows, full_width = gradient.shape[1:]
    side = stat_left.shape[-1]
    owners = lax.axis_size("fsdp")
    reps = lax.axis_size("rep")
    chips = reps // 2
    cols = full_width // side
    rows = shard_rows // reps
    share = side // reps
    quarters = side // shard_rows
    block_rows = owner_cols.shape[0]
    rep = lax.axis_index("rep")
    chip, core = rep // 2, rep % 2
    my_row = lax.axis_index("fsdp") // quarters
    ids = jnp.stack([rep, my_row]).astype(jnp.int32)
    oc = owner_cols[:, 0, :]
    barrier = lax.optimization_barrier

    grad = gradient[0].reshape(chips, 2, rows, full_width)
    swap = [(i, i ^ 1) for i in range(reps)]
    other = lax.ppermute(pick(grad, 1 - core, 1), "rep", swap)
    mine = pick(grad, core, 1)
    parts = []
    for k in range(chips):
        to = (chip + k) % chips
        piece = pick(mine, to) + pick(other, to)
        parts.append(piece if k == 0 else rep_shift(piece, 2 * k, reps))
    second = lax.dynamic_slice_in_dim(second_moment, rep * rows, rows, 0)
    later_ids, _ = barrier((ids, parts[0]))
    stats = (block_rows, share, side)
    pair = (2, share, side)
    root_pair = (2, share, 3 * side // 4)
    roots = shuffle(
        root_plan,
        [root_pair] * reps,
        [later_ids],
        [root_left[0, 0], root_right[0, 0]],
        6 * reps,
    )
    ids, *roots = barrier((ids, *roots))

    strip = (rows, full_width)
    tail = (8, side)
    moment, squares, packed = call(
        functools.partial(moment_kernel, cols, reps),
        [strip, tail, (owners, rows, side)],
        [ids, oc],
        [*parts, second],
        [pltpu.VMEM(strip, F32)],
    )
    lines = [[2 * x + c for x in range(chips)] for c in range(2)]
    moment_line = lax.all_gather(moment, "rep", axis=0, tiled=True, axis_index_groups=lines)
    packed, *roots = barrier((packed, *roots))
    arrived = lax.all_to_all(packed, "fsdp", 0, 0, tiled=True)
    roots = [r if k == 0 else rep_shift(r, k, reps) for k, r in enumerate(roots)]
    arrived, squares, *roots = barrier((arrived, squares, *roots))

    square_sum = squares
    for bits in (1, 2, 3):
        square_sum = square_sum + lax.ppermute(
            squares, "fsdp", [(i, i ^ bits) for i in range(owners)]
        )
    blocks = lax.all_to_all(
        arrived.reshape(block_rows, quarters, rows, side), "rep", 0, 0, tiled=True
    )
    half = pltpu.VMEM((side, side), BF16)
    full = pltpu.VMEM((side, side), F32)
    (applied,) = call(
        apply_kernel, [blocks.shape], [ids], [blocks, *roots], [half] * 2 + [full] * 3
    )
    spread = lax.all_to_all(applied, "rep", 0, 0, tiled=True)
    grams = call(
        gram_kernel,
        [(2 * share + 8, side)] * reps,
        [ids],
        [blocks, square_sum],
        [half] * 2 + [full] * 2,
    )
    spread, moment_line, *grams = barrier((spread, moment_line, *grams))
    moment_swap = lax.ppermute(moment_line, "rep", swap)
    returned = lax.all_to_all(spread.reshape(owners, rows, side), "fsdp", 0, 0, tiled=True)
    grams = [g if k == 0 else rep_shift(g, k, reps) for k, g in enumerate(grams)]
    returned, *grams = barrier((returned, *grams))
    middle = full_width // 2
    low, high = call(
        direction_kernel,
        [(rows, middle)] * 2,
        [ids, oc],
        [returned, *grams],
        [pltpu.VMEM(strip, F32), pltpu.VMEM((16, 128), F32)],
    )
    left_low = rep_shift(low, 2, reps)
    right_high = rep_shift(high, reps - 2, reps)
    left_high = rep_shift(high, 2, reps)
    right_low = rep_shift(low, reps - 2, reps)
    last_ids, left_low, right_high = barrier((ids, left_low, right_high))
    moment_new, left_new, right_new = call(
        stat_kernel,
        [(shard_rows, full_width), stats, stats],
        [last_ids],
        [moment_line, moment_swap, stat_left[0, 0], stat_right[0, 0], *grams],
        [],
    )
    far_low = rep_shift(left_low, 2, reps)
    far_high = rep_shift(right_high, reps - 2, reps)
    found = [low, high, left_low, left_high, right_low, right_high]
    swapped = [lax.ppermute(x, "rep", swap) for x in found]
    far_low, far_high, left_new = barrier((far_low, far_high, left_new))
    far = [far_low, far_high]
    far_swapped = [lax.ppermute(x, "rep", swap) for x in far]
    (direction,) = shuffle(
        place_plan,
        [(shard_rows, full_width)],
        [ids],
        [*found, *far, *swapped, *far_swapped],
        16,
    )
    return (direction, moment_new, left_new[None, None], right_new[None, None])


def solution(mesh):
    return jax.shard_map(
        shards,
        mesh=mesh,
        in_specs=(
            P("rep", "fsdp", None),
            P("fsdp", None),
            P(),
            P("fsdp", None, None, "rep", None),
            P("fsdp", None, None, "rep", None),
            P("fsdp", None, None, "rep", None),
            P("fsdp", None, None, "rep", None),
        ),
        out_specs=(
            P("fsdp", None),
            P("fsdp", None),
            P("fsdp", None, None, "rep", None),
            P("fsdp", None, None, "rep", None),
        ),
        check_vma=False,
    )
```

```python
import functools

import jax
import jax.numpy as jnp
from jax import lax
from jax.experimental import pallas as pl
from jax.experimental.pallas import tpu as pltpu
from jax.sharding import PartitionSpec as P

SHAMPOO_DECAY = 0.9
ADAM_DECAY = 0.95
ADAM_EPS = 1e-08
NORM_EPS = 1e-06
PARAMS = pltpu.CompilerParams(vmem_limit_bytes=32 * 1024 * 1024)
F32 = jnp.float32
BF16 = jnp.bfloat16


def rep_shift(value, step, count):
    return lax.ppermute(value, "rep", [(i, (i + step) % count) for i in range(count)])


def pick(array, index, axis=0):
    return lax.dynamic_index_in_dim(array, index, axis, keepdims=False)


def split(value):
    high = value.astype(BF16)
    return high, (value - high.astype(F32)).astype(BF16)


def dot3(a, b, dims):
    dot = functools.partial(
        lax.dot_general, dimension_numbers=(dims, ((), ())), preferred_element_type=F32
    )
    return dot(a[0], b[0]) + (dot(a[0], b[1]) + dot(a[1], b[0]))


def moment_kernel(cols, replicas, ids, owner_cols, *refs):
    parts, second = refs[:4], refs[4]
    moment, squares, packed, averaged = refs[5:]
    row = ids[1]
    width = packed.shape[-1]
    squares[...] = jnp.zeros_like(squares)
    for c in range(cols):
        here = slice(c * width, (c + 1) * width)
        summed = (parts[0][:, here] + parts[1][:, here]) + (parts[2][:, here] + parts[3][:, here])
        mean = summed / replicas
        averaged[:, here] = mean
        new = ADAM_DECAY * second[:, here] + (1.0 - ADAM_DECAY) * mean * mean
        moment[:, here] = new
        step = mean / (jnp.sqrt(new) + ADAM_EPS)
        square = jnp.sum(step * step, axis=0, keepdims=True)
        lanes = square[:, 0:128]
        for k in range(1, width // 128):
            lanes = lanes + square[:, k * 128 : (k + 1) * 128]
        lane = (c // 8) * 128
        squares[c % 8 : c % 8 + 1, lane : lane + 128] = lanes
    for o in range(packed.shape[0]):
        col = owner_cols[row, o]
        start = pl.multiple_of(jnp.maximum(col, 0) * width, width)
        piece = averaged[:, pl.ds(start, width)]
        packed[o] = jnp.where(col >= 0, piece, 0.0)


def load_block(blocks, high, low):
    pieces, quarters, rows, _ = blocks.shape
    for i in range(quarters):
        for r in range(pieces):
            at = (i * pieces + r) * rows
            high[at : at + rows, :], low[at : at + rows, :] = split(blocks[r, i])


def root_kernel(ids, *refs):
    roots = refs[:8]
    lh, ll, rh, rl, left, right = refs[8:]
    count, side = 8, left.shape[0]
    share = side // count
    part = side // 4
    for k in range(count):
        other = lax.rem(ids[0] - k + count, count)
        start = pl.multiple_of(other * share, share)
        for j in range(3):
            lane = pl.multiple_of(lax.rem(other // 2 + j, 4) * part, part)
            here = slice(j * part, (j + 1) * part)
            left[pl.ds(start, share), pl.ds(lane, part)] = roots[k][0, :, here]
            right[pl.ds(start, share), pl.ds(lane, part)] = roots[k][1, :, here]
    for x in range(4):
        before = (x + 3) % 4
        at, to = slice(x * part, (x + 1) * part), slice(before * part, (before + 1) * part)
        left[at, to] = left[to, at].T
        right[at, to] = right[to, at].T
    lh[...], ll[...] = split(left[...])
    rh[...], rl[...] = split(right[...])


def apply_kernel(blocks, lh, ll, rh, rl, applied, gh, gl, whole):
    load_block(blocks, gh, gl)
    product = dot3((gh[...], gl[...]), (rh[...], rl[...]), ((1,), (0,)))
    value = dot3((lh[...], ll[...]), split(product), ((1,), (0,)))
    whole[...] = value
    norm = jnp.sqrt(jnp.sum(value * value, keepdims=True))
    scale = 1.0 / (norm + NORM_EPS)
    pieces, quarters, rows, _ = applied.shape
    for i in range(quarters):
        for r in range(pieces):
            at = (i * pieces + r) * rows
            applied[r, i] = whole[at : at + rows, :] * scale


def gram_kernel(ids, blocks, squares, *refs):
    outs = refs[:8]
    gh, gl, left, right = refs[8:]
    count, side = 8, left.shape[0]
    share = side // count
    load_block(blocks, gh, gl)
    g = (gh[...], gl[...])
    left[...] = dot3(g, g, ((1,), (1,)))
    right[...] = dot3(g, g, ((0,), (0,)))
    for k in range(count):
        start = pl.multiple_of(lax.rem(ids[0] + k, count) * share, share)
        outs[k][0:share, :] = left[pl.ds(start, share), :]
        outs[k][share : 2 * share, :] = right[pl.ds(start, share), :]
        outs[k][2 * share :, :] = squares[...]


def stat_kernel(ids, own, swapped, stat_left, stat_right, *refs):
    grams = refs[:8]
    moment_new, left, right = refs[8:]
    core = lax.rem(ids[0], 2)
    rows = own.shape[0] // 4
    for x in range(4):
        here = slice(x * rows, (x + 1) * rows)
        at = pl.multiple_of((2 * x + core) * rows, rows)
        moment_new[pl.ds(at, rows), :] = own[here, :]
        at = pl.multiple_of((2 * x + 1 - core) * rows, rows)
        moment_new[pl.ds(at, rows), :] = swapped[here, :]
    share = left.shape[1]
    for k in range(8):
        b = lax.rem(ids[0] - k + 8, 8)
        left[b] = SHAMPOO_DECAY * stat_left[b] + (1.0 - SHAMPOO_DECAY) * grams[k][0:share, :]
        right[b] = (
            SHAMPOO_DECAY * stat_right[b] + (1.0 - SHAMPOO_DECAY) * grams[k][share : 2 * share, :]
        )


def direction_kernel(ids, owner_cols, returned, *refs):
    grams = refs[:8]
    direction, norms = refs[8:]
    row = ids[1]
    width = returned.shape[-1]
    total = grams[0][...]
    for k in range(1, 8):
        total = total + grams[k][...]
    for c in range(direction.shape[-1] // width):
        lane = (c // 8) * 128
        lanes = total[c % 8 : c % 8 + 1, lane : lane + 128]
        norm = jnp.sqrt(jnp.sum(lanes, axis=1, keepdims=True))
        norms[c : c + 1, :] = jnp.broadcast_to(norm, (1, 128))
    for o in range(returned.shape[0]):
        col = owner_cols[row, o]

        @pl.when(col >= 0)
        def _():
            norm = norms[pl.ds(col, 1), :][:, 0:1]
            start = pl.multiple_of(col * width, width)
            direction[:, pl.ds(start, width)] = returned[o] * norm


def staged(kernel, cuts, n_small, n_in, n_out, *refs):
    cut = [n_small, n_in, n_out, n_in, n_out]
    groups, at = [], 0
    for size in cut:
        groups.append(refs[at : at + size])
        at += size
    small, sources, targets, ins, outs = groups
    sources = [
        src if cut is None else src.at[pl.ds(*cut), :] for src, cut in zip(sources, cuts)
    ]
    in_sems, out_sems = refs[at : at + 2]
    loads = [
        pltpu.make_async_copy(src, dst, in_sems.at[i])
        for i, (src, dst) in enumerate(zip(sources, ins))
    ]
    for load in loads:
        load.start()
    for load in loads:
        load.wait()
    kernel(*small, *ins, *outs, *refs[at + 2 :])
    stores = [
        pltpu.make_async_copy(src, dst, out_sems.at[i])
        for i, (src, dst) in enumerate(zip(outs, targets))
    ]
    for store in stores:
        store.start()
    for store in stores:
        store.wait()


def call(kernel, outs, small, ins, scratch, cuts=None, dtype=F32):
    hbm = pl.BlockSpec(memory_space=pltpu.HBM)
    smem = pl.BlockSpec(memory_space=pltpu.SMEM)
    cuts = cuts or [None] * len(ins)
    held = [
        pltpu.VMEM(x.shape if cut is None else (cut[1], *x.shape[1:]), x.dtype)
        for x, cut in zip(ins, cuts)
    ]
    held = held + [pltpu.VMEM(s, dtype) for s in outs]
    sems = [pltpu.SemaphoreType.DMA((len(ins),)), pltpu.SemaphoreType.DMA((len(outs),))]
    return pl.pallas_call(
        functools.partial(staged, kernel, cuts, len(small), len(ins), len(outs)),
        out_shape=[pltpu.HBM(shape, dtype) for shape in outs],
        in_specs=[smem] * len(small) + [hbm] * len(ins),
        out_specs=[hbm] * len(outs),
        scratch_shapes=held + sems + scratch,
        compiler_params=PARAMS,
    )(*small, *[pltpu.with_memory_space_constraint(x, pltpu.HBM) for x in ins])


def root_plan(ids, ins, outs):
    chip = ids[0] // 2
    for k, out in enumerate(outs):
        to = lax.rem(ids[0] + k, 8)
        for side in range(2):
            for j in range(3):
                lane = pl.multiple_of(lax.rem(chip + j, 4) * 128, 128)
                yield (
                    ins[side].at[to, :, pl.ds(lane, 128)],
                    out.at[side, :, slice(j * 128, (j + 1) * 128)],
                )


def place_plan(ids, ins, outs):
    core = ids[0] % 2
    rows = ins[0].shape[0] // 4
    for x in range(4):
        for piece, owner in zip(ins, (core, 1 - core)):
            start = pl.multiple_of((x * 2 + owner) * rows, rows)
            yield piece.at[pl.ds(x * rows, rows), :], outs[0].at[pl.ds(start, rows), :]


def copying(plan, split_stores, n_small, n_in, n_out, *refs):
    small, ins = refs[:n_small], refs[n_small : n_small + n_in]
    outs = refs[n_small + n_in : n_small + n_in + n_out]
    held, (sems, out_sems) = refs[n_small + n_in + n_out : -2], refs[-2:]
    loads = [
        pltpu.make_async_copy(src, dst, sems.at[i])
        for i, (src, dst) in enumerate(plan(*small, ins, held))
    ]
    pairs = zip(held, outs)
    if split_stores:
        landed = [dst for _, dst in plan(*small, ins, held)]
        pairs = zip(landed, [dst for _, dst in plan(*small, ins, outs)])
    stores = [
        pltpu.make_async_copy(src, dst, out_sems.at[i]) for i, (src, dst) in enumerate(pairs)
    ]
    for load in loads:
        load.start()
    for i, load in enumerate(loads):
        load.wait()
        if split_stores:
            stores[i].start()
    if not split_stores:
        for store in stores:
            store.start()
    for store in stores:
        store.wait()


def shuffle(plan, outs, small, ins, count, split_stores=False):
    hbm = pl.BlockSpec(memory_space=pltpu.HBM)
    smem = pl.BlockSpec(memory_space=pltpu.SMEM)
    return pl.pallas_call(
        functools.partial(copying, plan, split_stores, len(small), len(ins), len(outs)),
        out_shape=[pltpu.HBM(shape, F32) for shape in outs],
        in_specs=[smem] * len(small) + [hbm] * len(ins),
        out_specs=[hbm] * len(outs),
        scratch_shapes=[pltpu.VMEM(shape, F32) for shape in outs]
        + [pltpu.SemaphoreType.DMA((count,))] * 2,
        compiler_params=PARAMS,
    )(*small, *[pltpu.with_memory_space_constraint(x, pltpu.HBM) for x in ins])


def shards(gradient, second_moment, owner_cols, stat_left, stat_right, root_left, root_right):
    shard_rows, full_width = gradient.shape[1:]
    side = stat_left.shape[-1]
    owners = lax.axis_size("fsdp")
    reps = lax.axis_size("rep")
    chips = reps // 2
    cols = full_width // side
    rows = shard_rows // reps
    share = side // reps
    quarters = side // shard_rows
    block_rows = owner_cols.shape[0]
    rep = lax.axis_index("rep")
    chip, core = rep // 2, rep % 2
    my_row = lax.axis_index("fsdp") // quarters
    ids = jnp.stack([rep, my_row]).astype(jnp.int32)
    oc = owner_cols[:, 0, :]
    barrier = lax.optimization_barrier

    grad = gradient[0].reshape(chips, 2, rows, full_width)
    swap = [(i, i ^ 1) for i in range(reps)]
    other = lax.ppermute(pick(grad, 1 - core, 1), "rep", swap)
    mine = pick(grad, core, 1)
    parts = []
    for k in range(chips):
        to = (chip + k) % chips
        piece = pick(mine, to) + pick(other, to)
        parts.append(piece if k == 0 else rep_shift(piece, 2 * k, reps))
    second = lax.dynamic_slice_in_dim(second_moment, rep * rows, rows, 0)
    later_ids, _ = barrier((ids, parts[0]))
    stats = (block_rows, share, side)
    pair = (2, share, side)
    root_pair = (2, share, 3 * side // 4)
    roots = shuffle(
        root_plan,
        [root_pair] * reps,
        [later_ids],
        [root_left[0, 0], root_right[0, 0]],
        6 * reps,
    )
    ids, *roots = barrier((ids, *roots))

    strip = (rows, full_width)
    tail = (8, side)
    moment, squares, packed = call(
        functools.partial(moment_kernel, cols, reps),
        [strip, tail, (owners, rows, side)],
        [ids, oc],
        [*parts, second],
        [pltpu.VMEM(strip, F32)],
    )
    lines = [[2 * x + c for x in range(chips)] for c in range(2)]
    moment_line = lax.all_gather(moment, "rep", axis=0, tiled=True, axis_index_groups=lines)
    packed, *roots = barrier((packed, *roots))
    arrived = lax.all_to_all(packed, "fsdp", 0, 0, tiled=True)
    roots = [r if k == 0 else rep_shift(r, k, reps) for k, r in enumerate(roots)]
    arrived, squares, *roots = barrier((arrived, squares, *roots))

    square_sum = squares
    for bits in (1, 2, 3):
        square_sum = square_sum + lax.ppermute(
            squares, "fsdp", [(i, i ^ bits) for i in range(owners)]
        )
    blocks = lax.all_to_all(
        arrived.reshape(block_rows, quarters, rows, side), "rep", 0, 0, tiled=True
    )
    half = pltpu.VMEM((side, side), BF16)
    full = pltpu.VMEM((side, side), F32)
    halves = call(
        root_kernel, [(side, side)] * 4, [ids], roots, [full] * 2, dtype=BF16
    )
    (applied,) = call(
        apply_kernel, [blocks.shape], [], [blocks, *halves], [half] * 2 + [full]
    )
    spread = lax.all_to_all(applied, "rep", 0, 0, tiled=True)
    grams = call(
        gram_kernel,
        [(2 * share + 8, side)] * reps,
        [ids],
        [blocks, square_sum],
        [half] * 2 + [full] * 2,
    )
    spread, moment_line, *grams = barrier((spread, moment_line, *grams))
    moment_swap = lax.ppermute(moment_line, "rep", swap)
    returned = lax.all_to_all(spread.reshape(owners, rows, side), "fsdp", 0, 0, tiled=True)
    grams = [g if k == 0 else rep_shift(g, k, reps) for k, g in enumerate(grams)]
    returned, *grams = barrier((returned, *grams))
    tails = (2 * share, 8)
    (part,) = call(
        direction_kernel,
        [strip],
        [ids, oc],
        [returned, *grams],
        [pltpu.VMEM((16, 128), F32)],
        [None] + [tails] * reps,
    )
    line = lax.all_gather(part, "rep", axis=0, tiled=True, axis_index_groups=lines)
    last_ids, part = barrier((ids, part))
    moment_new, left_new, right_new = call(
        stat_kernel,
        [(shard_rows, full_width), stats, stats],
        [last_ids],
        [moment_line, moment_swap, stat_left[0, 0], stat_right[0, 0], *grams],
        [],
    )
    line, left_new = barrier((line, left_new))
    (direction,) = shuffle(
        place_plan,
        [(shard_rows, full_width)],
        [ids],
        [line, lax.ppermute(line, "rep", swap)],
        2 * chips,
        True,
    )
    return (direction, moment_new, left_new[None, None], right_new[None, None])


def solution(mesh):
    return jax.shard_map(
        shards,
        mesh=mesh,
        in_specs=(
            P("rep", "fsdp", None),
            P("fsdp", None),
            P(),
            P("fsdp", None, None, "rep", None),
            P("fsdp", None, None, "rep", None),
            P("fsdp", None, None, "rep", None),
            P("fsdp", None, None, "rep", None),
        ),
        out_specs=(
            P("fsdp", None),
            P("fsdp", None),
            P("fsdp", None, None, "rep", None),
            P("fsdp", None, None, "rep", None),
        ),
        check_vma=False,
    )
```

```python
import functools

import jax
import jax.numpy as jnp
from jax import lax
from jax.experimental import pallas as pl
from jax.experimental.pallas import tpu as pltpu
from jax.sharding import PartitionSpec as P

SHAMPOO_DECAY = 0.9
ADAM_DECAY = 0.95
ADAM_EPS = 1e-08
NORM_EPS = 1e-06
PARAMS = pltpu.CompilerParams(vmem_limit_bytes=32 * 1024 * 1024)
F32 = jnp.float32
BF16 = jnp.bfloat16


def rep_shift(value, step, count):
    return lax.ppermute(value, "rep", [(i, (i + step) % count) for i in range(count)])


def pick(array, index, axis=0):
    return lax.dynamic_index_in_dim(array, index, axis, keepdims=False)


def split(value):
    high = value.astype(BF16)
    return high, (value - high.astype(F32)).astype(BF16)


def dot3(a, b, dims):
    dot = functools.partial(
        lax.dot_general, dimension_numbers=(dims, ((), ())), preferred_element_type=F32
    )
    return dot(a[0], b[0]) + (dot(a[0], b[1]) + dot(a[1], b[0]))


def moment_kernel(cols, replicas, ids, owner_cols, *refs):
    parts, second = refs[:4], refs[4]
    moment, squares, packed, averaged = refs[5:]
    row = ids[1]
    width = packed.shape[-1]
    squares[...] = jnp.zeros_like(squares)
    for c in range(cols):
        here = slice(c * width, (c + 1) * width)
        summed = (parts[0][:, here] + parts[1][:, here]) + (parts[2][:, here] + parts[3][:, here])
        mean = summed / replicas
        averaged[:, here] = mean
        new = ADAM_DECAY * second[:, here] + (1.0 - ADAM_DECAY) * mean * mean
        moment[:, here] = new
        step = mean / (jnp.sqrt(new) + ADAM_EPS)
        square = jnp.sum(step * step, axis=0, keepdims=True)
        lanes = square[:, 0:128]
        for k in range(1, width // 128):
            lanes = lanes + square[:, k * 128 : (k + 1) * 128]
        lane = (c // 8) * 128
        squares[c % 8 : c % 8 + 1, lane : lane + 128] = lanes
    for o in range(packed.shape[0]):
        col = owner_cols[row, o]
        start = pl.multiple_of(jnp.maximum(col, 0) * width, width)
        piece = averaged[:, pl.ds(start, width)]
        packed[o] = jnp.where(col >= 0, piece, 0.0)


def load_block(blocks, high, low):
    pieces, quarters, rows, _ = blocks.shape
    for i in range(quarters):
        for r in range(pieces):
            at = (i * pieces + r) * rows
            high[at : at + rows, :], low[at : at + rows, :] = split(blocks[r, i])


def root_kernel(ids, *refs):
    roots = refs[:8]
    lh, ll, rh, rl, left, right = refs[8:]
    count, side = 8, left.shape[0]
    share = side // count
    part = side // 4
    for k in range(count):
        other = lax.rem(ids[0] - k + count, count)
        start = pl.multiple_of(other * share, share)
        for j in range(3):
            lane = pl.multiple_of(lax.rem(other // 2 + j, 4) * part, part)
            here = slice(j * part, (j + 1) * part)
            left[pl.ds(start, share), pl.ds(lane, part)] = roots[k][0, :, here]
            right[pl.ds(start, share), pl.ds(lane, part)] = roots[k][1, :, here]
    for x in range(4):
        before = (x + 3) % 4
        at, to = slice(x * part, (x + 1) * part), slice(before * part, (before + 1) * part)
        left[at, to] = left[to, at].T
        right[at, to] = right[to, at].T
    lh[...], ll[...] = split(left[...])
    rh[...], rl[...] = split(right[...])


def apply_kernel(blocks, lh, ll, rh, rl, applied, gh, gl, whole):
    load_block(blocks, gh, gl)
    product = dot3((gh[...], gl[...]), (rh[...], rl[...]), ((1,), (0,)))
    value = dot3((lh[...], ll[...]), split(product), ((1,), (0,)))
    whole[...] = value
    norm = jnp.sqrt(jnp.sum(value * value, keepdims=True))
    scale = 1.0 / (norm + NORM_EPS)
    pieces, quarters, rows, _ = applied.shape
    for i in range(quarters):
        for r in range(pieces):
            at = (i * pieces + r) * rows
            applied[r, i] = whole[at : at + rows, :] * scale


def gram_kernel(ids, blocks, squares, *refs):
    outs = refs[:8]
    gh, gl, left, right = refs[8:]
    count, side = 8, left.shape[0]
    share = side // count
    load_block(blocks, gh, gl)
    g = (gh[...], gl[...])
    left[...] = dot3(g, g, ((1,), (1,)))
    right[...] = dot3(g, g, ((0,), (0,)))
    for k in range(count):
        start = pl.multiple_of(lax.rem(ids[0] + k, count) * share, share)
        outs[k][0:share, :] = left[pl.ds(start, share), :]
        outs[k][share : 2 * share, :] = right[pl.ds(start, share), :]
        outs[k][2 * share :, :] = squares[...]


def stat_kernel(ids, own, swapped, stat_left, stat_right, *refs):
    grams = refs[:8]
    moment_new, left, right = refs[8:]
    core = lax.rem(ids[0], 2)
    rows = own.shape[0] // 4
    for x in range(4):
        here = slice(x * rows, (x + 1) * rows)
        at = pl.multiple_of((2 * x + core) * rows, rows)
        moment_new[pl.ds(at, rows), :] = own[here, :]
        at = pl.multiple_of((2 * x + 1 - core) * rows, rows)
        moment_new[pl.ds(at, rows), :] = swapped[here, :]
    share = left.shape[1]
    for k in range(8):
        b = lax.rem(ids[0] - k + 8, 8)
        left[b] = SHAMPOO_DECAY * stat_left[b] + (1.0 - SHAMPOO_DECAY) * grams[k][0:share, :]
        right[b] = (
            SHAMPOO_DECAY * stat_right[b] + (1.0 - SHAMPOO_DECAY) * grams[k][share : 2 * share, :]
        )


def direction_kernel(ids, owner_cols, returned, *refs):
    grams = refs[:8]
    direction, norms = refs[8:]
    row = ids[1]
    width = returned.shape[-1]
    total = grams[0][...]
    for k in range(1, 8):
        total = total + grams[k][...]
    for c in range(direction.shape[-1] // width):
        lane = (c // 8) * 128
        lanes = total[c % 8 : c % 8 + 1, lane : lane + 128]
        norm = jnp.sqrt(jnp.sum(lanes, axis=1, keepdims=True))
        norms[c : c + 1, :] = jnp.broadcast_to(norm, (1, 128))
    for o in range(returned.shape[0]):
        col = owner_cols[row, o]

        @pl.when(col >= 0)
        def _():
            norm = norms[pl.ds(col, 1), :][:, 0:1]
            start = pl.multiple_of(col * width, width)
            direction[:, pl.ds(start, width)] = returned[o] * norm


def staged(kernel, cuts, n_small, n_in, n_out, *refs):
    cut = [n_small, n_in, n_out, n_in, n_out]
    groups, at = [], 0
    for size in cut:
        groups.append(refs[at : at + size])
        at += size
    small, sources, targets, ins, outs = groups
    sources = [
        src if cut is None else src.at[pl.ds(*cut), :] for src, cut in zip(sources, cuts)
    ]
    in_sems, out_sems = refs[at : at + 2]
    loads = [
        pltpu.make_async_copy(src, dst, in_sems.at[i])
        for i, (src, dst) in enumerate(zip(sources, ins))
    ]
    for load in loads:
        load.start()
    for load in loads:
        load.wait()
    kernel(*small, *ins, *outs, *refs[at + 2 :])
    stores = [
        pltpu.make_async_copy(src, dst, out_sems.at[i])
        for i, (src, dst) in enumerate(zip(outs, targets))
    ]
    for store in stores:
        store.start()
    for store in stores:
        store.wait()


def call(kernel, outs, small, ins, scratch, cuts=None, dtype=F32):
    hbm = pl.BlockSpec(memory_space=pltpu.HBM)
    smem = pl.BlockSpec(memory_space=pltpu.SMEM)
    cuts = cuts or [None] * len(ins)
    held = [
        pltpu.VMEM(x.shape if cut is None else (cut[1], *x.shape[1:]), x.dtype)
        for x, cut in zip(ins, cuts)
    ]
    held = held + [pltpu.VMEM(s, dtype) for s in outs]
    sems = [pltpu.SemaphoreType.DMA((len(ins),)), pltpu.SemaphoreType.DMA((len(outs),))]
    return pl.pallas_call(
        functools.partial(staged, kernel, cuts, len(small), len(ins), len(outs)),
        out_shape=[pltpu.HBM(shape, dtype) for shape in outs],
        in_specs=[smem] * len(small) + [hbm] * len(ins),
        out_specs=[hbm] * len(outs),
        scratch_shapes=held + sems + scratch,
        compiler_params=PARAMS,
    )(*small, *[pltpu.with_memory_space_constraint(x, pltpu.HBM) for x in ins])


def root_plan(ids, ins, outs):
    chip = ids[0] // 2
    for k, out in enumerate(outs):
        to = lax.rem(ids[0] + k, 8)
        for side in range(2):
            for j in range(3):
                lane = pl.multiple_of(lax.rem(chip + j, 4) * 128, 128)
                yield (
                    ins[side].at[to, :, pl.ds(lane, 128)],
                    out.at[side, :, slice(j * 128, (j + 1) * 128)],
                )


def place_plan(ids, ins, outs):
    chip, core = ids[0] // 2, ids[0] % 2
    rows = ins[0].shape[0]
    for j, piece in enumerate(ins):
        owner = core if j < 4 else 1 - core
        start = pl.multiple_of((lax.rem(chip - j % 4 + 4, 4) * 2 + owner) * rows, rows)
        yield piece, outs[0].at[pl.ds(start, rows), :]


def copying(plan, split_stores, n_small, n_in, n_out, *refs):
    small, ins = refs[:n_small], refs[n_small : n_small + n_in]
    outs = refs[n_small + n_in : n_small + n_in + n_out]
    held, (sems, out_sems) = refs[n_small + n_in + n_out : -2], refs[-2:]
    loads = [
        pltpu.make_async_copy(src, dst, sems.at[i])
        for i, (src, dst) in enumerate(plan(*small, ins, held))
    ]
    pairs = zip(held, outs)
    if split_stores:
        landed = [dst for _, dst in plan(*small, ins, held)]
        pairs = zip(landed, [dst for _, dst in plan(*small, ins, outs)])
    stores = [
        pltpu.make_async_copy(src, dst, out_sems.at[i]) for i, (src, dst) in enumerate(pairs)
    ]
    for load in loads:
        load.start()
    for i, load in enumerate(loads):
        load.wait()
        if split_stores:
            stores[i].start()
    if not split_stores:
        for store in stores:
            store.start()
    for store in stores:
        store.wait()


def shuffle(plan, outs, small, ins, count, split_stores=False):
    hbm = pl.BlockSpec(memory_space=pltpu.HBM)
    smem = pl.BlockSpec(memory_space=pltpu.SMEM)
    return pl.pallas_call(
        functools.partial(copying, plan, split_stores, len(small), len(ins), len(outs)),
        out_shape=[pltpu.HBM(shape, F32) for shape in outs],
        in_specs=[smem] * len(small) + [hbm] * len(ins),
        out_specs=[hbm] * len(outs),
        scratch_shapes=[pltpu.VMEM(shape, F32) for shape in outs]
        + [pltpu.SemaphoreType.DMA((count,))] * 2,
        compiler_params=PARAMS,
    )(*small, *[pltpu.with_memory_space_constraint(x, pltpu.HBM) for x in ins])


def shards(gradient, second_moment, owner_cols, stat_left, stat_right, root_left, root_right):
    shard_rows, full_width = gradient.shape[1:]
    side = stat_left.shape[-1]
    owners = lax.axis_size("fsdp")
    reps = lax.axis_size("rep")
    chips = reps // 2
    cols = full_width // side
    rows = shard_rows // reps
    share = side // reps
    quarters = side // shard_rows
    block_rows = owner_cols.shape[0]
    rep = lax.axis_index("rep")
    chip, core = rep // 2, rep % 2
    my_row = lax.axis_index("fsdp") // quarters
    ids = jnp.stack([rep, my_row]).astype(jnp.int32)
    oc = owner_cols[:, 0, :]
    barrier = lax.optimization_barrier

    grad = gradient[0].reshape(chips, 2, rows, full_width)
    swap = [(i, i ^ 1) for i in range(reps)]
    other = lax.ppermute(pick(grad, 1 - core, 1), "rep", swap)
    mine = pick(grad, core, 1)
    parts = []
    for k in range(chips):
        to = (chip + k) % chips
        piece = pick(mine, to) + pick(other, to)
        parts.append(piece if k == 0 else rep_shift(piece, 2 * k, reps))
    second = lax.dynamic_slice_in_dim(second_moment, rep * rows, rows, 0)
    later_ids, _ = barrier((ids, parts[0]))
    stats = (block_rows, share, side)
    pair = (2, share, side)
    root_pair = (2, share, 3 * side // 4)
    roots = shuffle(
        root_plan,
        [root_pair] * reps,
        [later_ids],
        [root_left[0, 0], root_right[0, 0]],
        6 * reps,
    )
    ids, *roots = barrier((ids, *roots))

    strip = (rows, full_width)
    tail = (8, side)
    moment, squares, packed = call(
        functools.partial(moment_kernel, cols, reps),
        [strip, tail, (owners, rows, side)],
        [ids, oc],
        [*parts, second],
        [pltpu.VMEM(strip, F32)],
    )
    lines = [[2 * x + c for x in range(chips)] for c in range(2)]
    moment_line = lax.all_gather(moment, "rep", axis=0, tiled=True, axis_index_groups=lines)
    packed, *roots = barrier((packed, *roots))
    arrived = lax.all_to_all(packed, "fsdp", 0, 0, tiled=True)
    roots = [r if k == 0 else rep_shift(r, k, reps) for k, r in enumerate(roots)]
    arrived, squares, *roots = barrier((arrived, squares, *roots))

    square_sum = squares
    for bits in (1, 2, 3):
        square_sum = square_sum + lax.ppermute(
            squares, "fsdp", [(i, i ^ bits) for i in range(owners)]
        )
    blocks = lax.all_to_all(
        arrived.reshape(block_rows, quarters, rows, side), "rep", 0, 0, tiled=True
    )
    half = pltpu.VMEM((side, side), BF16)
    full = pltpu.VMEM((side, side), F32)
    halves = call(
        root_kernel, [(side, side)] * 4, [ids], roots, [full] * 2, dtype=BF16
    )
    (applied,) = call(
        apply_kernel, [blocks.shape], [], [blocks, *halves], [half] * 2 + [full]
    )
    spread = lax.all_to_all(applied, "rep", 0, 0, tiled=True)
    grams = call(
        gram_kernel,
        [(2 * share + 8, side)] * reps,
        [ids],
        [blocks, square_sum],
        [half] * 2 + [full] * 2,
    )
    spread, moment_line, *grams = barrier((spread, moment_line, *grams))
    moment_swap = lax.ppermute(moment_line, "rep", swap)
    returned = lax.all_to_all(spread.reshape(owners, rows, side), "fsdp", 0, 0, tiled=True)
    grams = [g if k == 0 else rep_shift(g, k, reps) for k, g in enumerate(grams)]
    returned, moment_swap, *grams = barrier((returned, moment_swap, *grams))
    tails = (2 * share, 8)
    (part,) = call(
        direction_kernel,
        [strip],
        [ids, oc],
        [returned, *grams],
        [pltpu.VMEM((16, 128), F32)],
        [None] + [tails] * reps,
    )
    found = [part] + [rep_shift(part, 2 * k, reps) for k in range(1, chips)]
    last_ids, _ = barrier((ids, part))
    moment_new, left_new, right_new = call(
        stat_kernel,
        [(shard_rows, full_width), stats, stats],
        [last_ids],
        [moment_line, moment_swap, stat_left[0, 0], stat_right[0, 0], *grams],
        [],
    )
    found[2], left_new = barrier((found[2], left_new))
    swapped = [lax.ppermute(x, "rep", swap) for x in found]
    (direction,) = shuffle(
        place_plan,
        [(shard_rows, full_width)],
        [ids],
        found + swapped,
        2 * chips,
        True,
    )
    return (direction, moment_new, left_new[None, None], right_new[None, None])


def solution(mesh):
    return jax.shard_map(
        shards,
        mesh=mesh,
        in_specs=(
            P("rep", "fsdp", None),
            P("fsdp", None),
            P(),
            P("fsdp", None, None, "rep", None),
            P("fsdp", None, None, "rep", None),
            P("fsdp", None, None, "rep", None),
            P("fsdp", None, None, "rep", None),
        ),
        out_specs=(
            P("fsdp", None),
            P("fsdp", None),
            P("fsdp", None, None, "rep", None),
            P("fsdp", None, None, "rep", None),
        ),
        check_vma=False,
    )
```

```python
import functools

import jax
import jax.numpy as jnp
from jax import lax
from jax.experimental import pallas as pl
from jax.experimental.pallas import tpu as pltpu
from jax.sharding import PartitionSpec as P

SHAMPOO_DECAY = 0.9
ADAM_DECAY = 0.95
ADAM_EPS = 1e-08
NORM_EPS = 1e-06
PARAMS = pltpu.CompilerParams(vmem_limit_bytes=32 * 1024 * 1024)
F32 = jnp.float32
BF16 = jnp.bfloat16


def rep_shift(value, step, count):
    return lax.ppermute(value, "rep", [(i, (i + step) % count) for i in range(count)])


def pick(array, index, axis=0):
    return lax.dynamic_index_in_dim(array, index, axis, keepdims=False)


def split(value):
    high = value.astype(BF16)
    return high, (value - high.astype(F32)).astype(BF16)


def dot3(a, b, dims):
    dot = functools.partial(
        lax.dot_general, dimension_numbers=(dims, ((), ())), preferred_element_type=F32
    )
    return dot(a[0], b[0]) + (dot(a[0], b[1]) + dot(a[1], b[0]))


def moment_kernel(cols, replicas, ids, owner_cols, *refs):
    parts, second = refs[:4], refs[4]
    moment, squares, packed, averaged = refs[5:]
    row = ids[1]
    width = packed.shape[-1]
    squares[...] = jnp.zeros_like(squares)
    for c in range(cols):
        here = slice(c * width, (c + 1) * width)
        summed = (parts[0][:, here] + parts[1][:, here]) + (parts[2][:, here] + parts[3][:, here])
        mean = summed / replicas
        averaged[:, here] = mean
        new = ADAM_DECAY * second[:, here] + (1.0 - ADAM_DECAY) * mean * mean
        moment[:, here] = new
        step = mean / (jnp.sqrt(new) + ADAM_EPS)
        square = jnp.sum(step * step, axis=0, keepdims=True)
        lanes = square[:, 0:128]
        for k in range(1, width // 128):
            lanes = lanes + square[:, k * 128 : (k + 1) * 128]
        lane = (c // 8) * 128
        squares[c % 8 : c % 8 + 1, lane : lane + 128] = lanes
    for o in range(packed.shape[0]):
        col = owner_cols[row, o]
        start = pl.multiple_of(jnp.maximum(col, 0) * width, width)
        piece = averaged[:, pl.ds(start, width)]
        packed[o] = jnp.where(col >= 0, piece, 0.0)


def load_block(blocks, high, low):
    pieces, quarters, rows, _ = blocks.shape
    for i in range(quarters):
        for r in range(pieces):
            at = (i * pieces + r) * rows
            high[at : at + rows, :], low[at : at + rows, :] = split(blocks[r, i])


def root_kernel(ids, *refs):
    roots = refs[:8]
    lh, ll, rh, rl, left, right = refs[8:]
    count, side = 8, left.shape[0]
    share = side // count
    part = side // 4
    for k in range(count):
        other = lax.rem(ids[0] - k + count, count)
        start = pl.multiple_of(other * share, share)
        for j in range(3):
            lane = pl.multiple_of(lax.rem(other // 2 + j, 4) * part, part)
            here = slice(j * part, (j + 1) * part)
            left[pl.ds(start, share), pl.ds(lane, part)] = roots[k][0, :, here]
            right[pl.ds(start, share), pl.ds(lane, part)] = roots[k][1, :, here]
    for x in range(4):
        before = (x + 3) % 4
        at, to = slice(x * part, (x + 1) * part), slice(before * part, (before + 1) * part)
        left[at, to] = left[to, at].T
        right[at, to] = right[to, at].T
    lh[...], ll[...] = split(left[...])
    rh[...], rl[...] = split(right[...])


def apply_kernel(blocks, lh, ll, rh, rl, applied, gh, gl, whole):
    load_block(blocks, gh, gl)
    product = dot3((gh[...], gl[...]), (rh[...], rl[...]), ((1,), (0,)))
    value = dot3((lh[...], ll[...]), split(product), ((1,), (0,)))
    whole[...] = value
    norm = jnp.sqrt(jnp.sum(value * value, keepdims=True))
    scale = 1.0 / (norm + NORM_EPS)
    pieces, quarters, rows, _ = applied.shape
    for i in range(quarters):
        for r in range(pieces):
            at = (i * pieces + r) * rows
            applied[r, i] = whole[at : at + rows, :] * scale


def gram_kernel(ids, blocks, squares, *refs):
    outs = refs[:8]
    gh, gl, left, right = refs[8:]
    count, side = 8, left.shape[0]
    share = side // count
    load_block(blocks, gh, gl)
    g = (gh[...], gl[...])
    left[...] = dot3(g, g, ((1,), (1,)))
    right[...] = dot3(g, g, ((0,), (0,)))
    for k in range(count):
        start = pl.multiple_of(lax.rem(ids[0] + k, count) * share, share)
        outs[k][0:share, :] = left[pl.ds(start, share), :]
        outs[k][share : 2 * share, :] = right[pl.ds(start, share), :]
        outs[k][2 * share :, :] = squares[...]


def stat_kernel(ids, own, swapped, stat_left, stat_right, *refs):
    grams = refs[:8]
    moment_new, left, right = refs[8:]
    core = lax.rem(ids[0], 2)
    rows = own.shape[0] // 4
    for x in range(4):
        here = slice(x * rows, (x + 1) * rows)
        at = pl.multiple_of((2 * x + core) * rows, rows)
        moment_new[pl.ds(at, rows), :] = own[here, :]
        at = pl.multiple_of((2 * x + 1 - core) * rows, rows)
        moment_new[pl.ds(at, rows), :] = swapped[here, :]
    share = left.shape[1]
    for k in range(8):
        b = lax.rem(ids[0] - k + 8, 8)
        left[b] = SHAMPOO_DECAY * stat_left[b] + (1.0 - SHAMPOO_DECAY) * grams[k][0:share, :]
        right[b] = (
            SHAMPOO_DECAY * stat_right[b] + (1.0 - SHAMPOO_DECAY) * grams[k][share : 2 * share, :]
        )


def direction_kernel(ids, owner_cols, returned, *refs):
    grams = refs[:8]
    direction, norms = refs[8:]
    row = ids[1]
    width = returned.shape[-1]
    total = grams[0][...]
    for k in range(1, 8):
        total = total + grams[k][...]
    for c in range(direction.shape[-1] // width):
        lane = (c // 8) * 128
        lanes = total[c % 8 : c % 8 + 1, lane : lane + 128]
        norm = jnp.sqrt(jnp.sum(lanes, axis=1, keepdims=True))
        norms[c : c + 1, :] = jnp.broadcast_to(norm, (1, 128))
    for o in range(returned.shape[0]):
        col = owner_cols[row, o]

        @pl.when(col >= 0)
        def _():
            norm = norms[pl.ds(col, 1), :][:, 0:1]
            start = pl.multiple_of(col * width, width)
            direction[:, pl.ds(start, width)] = returned[o] * norm


def staged(kernel, cuts, n_small, n_in, n_out, *refs):
    cut = [n_small, n_in, n_out, n_in, n_out]
    groups, at = [], 0
    for size in cut:
        groups.append(refs[at : at + size])
        at += size
    small, sources, targets, ins, outs = groups
    sources = [
        src if cut is None else src.at[pl.ds(*cut), :] for src, cut in zip(sources, cuts)
    ]
    in_sems, out_sems = refs[at : at + 2]
    loads = [
        pltpu.make_async_copy(src, dst, in_sems.at[i])
        for i, (src, dst) in enumerate(zip(sources, ins))
    ]
    for load in loads:
        load.start()
    for load in loads:
        load.wait()
    kernel(*small, *ins, *outs, *refs[at + 2 :])
    stores = [
        pltpu.make_async_copy(src, dst, out_sems.at[i])
        for i, (src, dst) in enumerate(zip(outs, targets))
    ]
    for store in stores:
        store.start()
    for store in stores:
        store.wait()


def call(kernel, outs, small, ins, scratch, cuts=None, dtype=F32):
    hbm = pl.BlockSpec(memory_space=pltpu.HBM)
    smem = pl.BlockSpec(memory_space=pltpu.SMEM)
    cuts = cuts or [None] * len(ins)
    held = [
        pltpu.VMEM(x.shape if cut is None else (cut[1], *x.shape[1:]), x.dtype)
        for x, cut in zip(ins, cuts)
    ]
    held = held + [pltpu.VMEM(s, dtype) for s in outs]
    sems = [pltpu.SemaphoreType.DMA((len(ins),)), pltpu.SemaphoreType.DMA((len(outs),))]
    return pl.pallas_call(
        functools.partial(staged, kernel, cuts, len(small), len(ins), len(outs)),
        out_shape=[pltpu.HBM(shape, dtype) for shape in outs],
        in_specs=[smem] * len(small) + [hbm] * len(ins),
        out_specs=[hbm] * len(outs),
        scratch_shapes=held + sems + scratch,
        compiler_params=PARAMS,
    )(*small, *[pltpu.with_memory_space_constraint(x, pltpu.HBM) for x in ins])


def root_plan(ids, ins, outs):
    chip = ids[0] // 2
    for k, out in enumerate(outs):
        to = lax.rem(ids[0] + k, 8)
        for side in range(2):
            for j in range(3):
                lane = pl.multiple_of(lax.rem(chip + j, 4) * 128, 128)
                yield (
                    ins[side].at[to, :, pl.ds(lane, 128)],
                    out.at[side, :, slice(j * 128, (j + 1) * 128)],
                )


def place_plan(ids, ins, outs):
    chip, core = ids[0] // 2, ids[0] % 2
    rows = ins[0].shape[0]
    for j, piece in enumerate(ins):
        owner = core if j < 4 else 1 - core
        start = pl.multiple_of((lax.rem(chip - j % 4 + 4, 4) * 2 + owner) * rows, rows)
        yield piece, outs[0].at[pl.ds(start, rows), :]


def copying(plan, split_stores, n_small, n_in, n_out, *refs):
    small, ins = refs[:n_small], refs[n_small : n_small + n_in]
    outs = refs[n_small + n_in : n_small + n_in + n_out]
    held, (sems, out_sems) = refs[n_small + n_in + n_out : -2], refs[-2:]
    loads = [
        pltpu.make_async_copy(src, dst, sems.at[i])
        for i, (src, dst) in enumerate(plan(*small, ins, held))
    ]
    pairs = zip(held, outs)
    if split_stores:
        landed = [dst for _, dst in plan(*small, ins, held)]
        pairs = zip(landed, [dst for _, dst in plan(*small, ins, outs)])
    stores = [
        pltpu.make_async_copy(src, dst, out_sems.at[i]) for i, (src, dst) in enumerate(pairs)
    ]
    for load in loads:
        load.start()
    for i, load in enumerate(loads):
        load.wait()
        if split_stores:
            stores[i].start()
    if not split_stores:
        for store in stores:
            store.start()
    for store in stores:
        store.wait()


def shuffle(plan, outs, small, ins, count, split_stores=False):
    hbm = pl.BlockSpec(memory_space=pltpu.HBM)
    smem = pl.BlockSpec(memory_space=pltpu.SMEM)
    return pl.pallas_call(
        functools.partial(copying, plan, split_stores, len(small), len(ins), len(outs)),
        out_shape=[pltpu.HBM(shape, F32) for shape in outs],
        in_specs=[smem] * len(small) + [hbm] * len(ins),
        out_specs=[hbm] * len(outs),
        scratch_shapes=[pltpu.VMEM(shape, F32) for shape in outs]
        + [pltpu.SemaphoreType.DMA((count,))] * 2,
        compiler_params=PARAMS,
    )(*small, *[pltpu.with_memory_space_constraint(x, pltpu.HBM) for x in ins])


def give_plan(ids, ins, outs):
    core = ids[0] % 2
    for x in range(ins[0].shape[0]):
        yield ins[0].at[x, 1 - core], outs[0].at[x]


def sum_kernel(ids, grad, other, *refs):
    outs, (mine, theirs, sems, out_sems) = refs[:4], refs[4:]
    chip, core = ids[0] // 2, ids[0] % 2
    order = (2, 1, 3, 0)
    loads, stores = {}, []
    for k in order:
        x = lax.rem(chip + k, 4)
        loads[k] = (
            pltpu.make_async_copy(grad.at[x, core], mine.at[k], sems.at[k]),
            pltpu.make_async_copy(other.at[x], theirs.at[k], sems.at[4 + k]),
        )
        for load in loads[k]:
            load.start()
    for k in order:
        for load in loads[k]:
            load.wait()
        mine[k] = mine[k] + theirs[k]
        stores.append(pltpu.make_async_copy(mine.at[k], outs[k], out_sems.at[k]))
        stores[-1].start()
    for store in stores:
        store.wait()


def pair_sums(ids, grad, other):
    hbm = pl.BlockSpec(memory_space=pltpu.HBM)
    chips, _, rows, width = grad.shape
    held = pltpu.VMEM((chips, rows, width), F32)
    return pl.pallas_call(
        sum_kernel,
        out_shape=[pltpu.HBM((rows, width), F32)] * chips,
        in_specs=[pl.BlockSpec(memory_space=pltpu.SMEM), hbm, hbm],
        out_specs=[hbm] * chips,
        scratch_shapes=[held, held]
        + [pltpu.SemaphoreType.DMA((2 * chips,)), pltpu.SemaphoreType.DMA((chips,))],
        compiler_params=PARAMS,
    )(ids, *[pltpu.with_memory_space_constraint(x, pltpu.HBM) for x in (grad, other)])


def shards(gradient, second_moment, owner_cols, stat_left, stat_right, root_left, root_right):
    shard_rows, full_width = gradient.shape[1:]
    side = stat_left.shape[-1]
    owners = lax.axis_size("fsdp")
    reps = lax.axis_size("rep")
    chips = reps // 2
    cols = full_width // side
    rows = shard_rows // reps
    share = side // reps
    quarters = side // shard_rows
    block_rows = owner_cols.shape[0]
    rep = lax.axis_index("rep")
    chip, core = rep // 2, rep % 2
    my_row = lax.axis_index("fsdp") // quarters
    ids = jnp.stack([rep, my_row]).astype(jnp.int32)
    oc = owner_cols[:, 0, :]
    barrier = lax.optimization_barrier

    grad = gradient[0].reshape(chips, 2, rows, full_width)
    swap = [(i, i ^ 1) for i in range(reps)]
    (given,) = shuffle(give_plan, [(chips, rows, full_width)], [ids], [grad], chips, True)
    other = lax.ppermute(given, "rep", swap)
    parts = pair_sums(ids, grad, other)
    parts = [p if k == 0 else rep_shift(p, 2 * k, reps) for k, p in enumerate(parts)]
    second = lax.dynamic_slice_in_dim(second_moment, rep * rows, rows, 0)
    later_ids, _ = barrier((ids, parts[0]))
    stats = (block_rows, share, side)
    pair = (2, share, side)
    root_pair = (2, share, 3 * side // 4)
    roots = shuffle(
        root_plan,
        [root_pair] * reps,
        [later_ids],
        [root_left[0, 0], root_right[0, 0]],
        6 * reps,
    )
    ids, *roots = barrier((ids, *roots))

    strip = (rows, full_width)
    tail = (8, side)
    moment, squares, packed = call(
        functools.partial(moment_kernel, cols, reps),
        [strip, tail, (owners, rows, side)],
        [ids, oc],
        [*parts, second],
        [pltpu.VMEM(strip, F32)],
    )
    lines = [[2 * x + c for x in range(chips)] for c in range(2)]
    moment_line = lax.all_gather(moment, "rep", axis=0, tiled=True, axis_index_groups=lines)
    packed, *roots = barrier((packed, *roots))
    arrived = lax.all_to_all(packed, "fsdp", 0, 0, tiled=True)
    roots = [r if k == 0 else rep_shift(r, k, reps) for k, r in enumerate(roots)]
    arrived, squares, *roots = barrier((arrived, squares, *roots))

    square_sum = squares
    for bits in (1, 2, 3):
        square_sum = square_sum + lax.ppermute(
            squares, "fsdp", [(i, i ^ bits) for i in range(owners)]
        )
    blocks = lax.all_to_all(
        arrived.reshape(block_rows, quarters, rows, side), "rep", 0, 0, tiled=True
    )
    half = pltpu.VMEM((side, side), BF16)
    full = pltpu.VMEM((side, side), F32)
    halves = call(
        root_kernel, [(side, side)] * 4, [ids], roots, [full] * 2, dtype=BF16
    )
    (applied,) = call(
        apply_kernel, [blocks.shape], [], [blocks, *halves], [half] * 2 + [full]
    )
    spread = lax.all_to_all(applied, "rep", 0, 0, tiled=True)
    grams = call(
        gram_kernel,
        [(2 * share + 8, side)] * reps,
        [ids],
        [blocks, square_sum],
        [half] * 2 + [full] * 2,
    )
    spread, moment_line, *grams = barrier((spread, moment_line, *grams))
    moment_swap = lax.ppermute(moment_line, "rep", swap)
    returned = lax.all_to_all(spread.reshape(owners, rows, side), "fsdp", 0, 0, tiled=True)
    grams = [g if k == 0 else rep_shift(g, k, reps) for k, g in enumerate(grams)]
    returned, moment_swap, *grams = barrier((returned, moment_swap, *grams))
    tails = (2 * share, 8)
    (part,) = call(
        direction_kernel,
        [strip],
        [ids, oc],
        [returned, *grams],
        [pltpu.VMEM((16, 128), F32)],
        [None] + [tails] * reps,
    )
    found = [part] + [rep_shift(part, 2 * k, reps) for k in range(1, chips)]
    last_ids, _ = barrier((ids, part))
    moment_new, left_new, right_new = call(
        stat_kernel,
        [(shard_rows, full_width), stats, stats],
        [last_ids],
        [moment_line, moment_swap, stat_left[0, 0], stat_right[0, 0], *grams],
        [],
    )
    found[2], left_new = barrier((found[2], left_new))
    swapped = [lax.ppermute(x, "rep", swap) for x in found]
    (direction,) = shuffle(
        place_plan,
        [(shard_rows, full_width)],
        [ids],
        found + swapped,
        2 * chips,
        True,
    )
    return (direction, moment_new, left_new[None, None], right_new[None, None])


def solution(mesh):
    return jax.shard_map(
        shards,
        mesh=mesh,
        in_specs=(
            P("rep", "fsdp", None),
            P("fsdp", None),
            P(),
            P("fsdp", None, None, "rep", None),
            P("fsdp", None, None, "rep", None),
            P("fsdp", None, None, "rep", None),
            P("fsdp", None, None, "rep", None),
        ),
        out_specs=(
            P("fsdp", None),
            P("fsdp", None),
            P("fsdp", None, None, "rep", None),
            P("fsdp", None, None, "rep", None),
        ),
        check_vma=False,
    )
```

```python
import functools

import jax
import jax.numpy as jnp
from jax import lax
from jax.experimental import pallas as pl
from jax.experimental.pallas import tpu as pltpu
from jax.sharding import PartitionSpec as P

SHAMPOO_DECAY = 0.9
ADAM_DECAY = 0.95
ADAM_EPS = 1e-08
NORM_EPS = 1e-06
PARAMS = pltpu.CompilerParams(vmem_limit_bytes=32 * 1024 * 1024)
F32 = jnp.float32
BF16 = jnp.bfloat16


def rep_shift(value, step, count):
    return lax.ppermute(value, "rep", [(i, (i + step) % count) for i in range(count)])


def pick(array, index, axis=0):
    return lax.dynamic_index_in_dim(array, index, axis, keepdims=False)


def split(value):
    high = value.astype(BF16)
    return high, (value - high.astype(F32)).astype(BF16)


def dot3(a, b, dims):
    dot = functools.partial(
        lax.dot_general, dimension_numbers=(dims, ((), ())), preferred_element_type=F32
    )
    return dot(a[0], b[0]) + (dot(a[0], b[1]) + dot(a[1], b[0]))


def moment_kernel(cols, replicas, ids, owner_cols, *refs):
    parts, second = refs[:4], refs[4]
    moment, squares, packed, averaged = refs[5:]
    row = ids[1]
    width = packed.shape[-1]
    squares[...] = jnp.zeros_like(squares)
    for c in range(cols):
        here = slice(c * width, (c + 1) * width)
        summed = (parts[0][:, here] + parts[1][:, here]) + (parts[2][:, here] + parts[3][:, here])
        mean = summed / replicas
        averaged[:, here] = mean
        new = ADAM_DECAY * second[:, here] + (1.0 - ADAM_DECAY) * mean * mean
        moment[:, here] = new
        step = mean / (jnp.sqrt(new) + ADAM_EPS)
        square = jnp.sum(step * step, axis=0, keepdims=True)
        lanes = square[:, 0:128]
        for k in range(1, width // 128):
            lanes = lanes + square[:, k * 128 : (k + 1) * 128]
        lane = (c // 8) * 128
        squares[c % 8 : c % 8 + 1, lane : lane + 128] = lanes
    for o in range(packed.shape[0]):
        col = owner_cols[row, o]
        start = pl.multiple_of(jnp.maximum(col, 0) * width, width)
        piece = averaged[:, pl.ds(start, width)]
        packed[o] = jnp.where(col >= 0, piece, 0.0)


def load_block(blocks, high, low):
    pieces, quarters, rows, _ = blocks.shape
    for i in range(quarters):
        for r in range(pieces):
            at = (i * pieces + r) * rows
            high[at : at + rows, :], low[at : at + rows, :] = split(blocks[r, i])


def root_kernel(ids, *refs):
    roots = refs[:8]
    lh, ll, rh, rl, left, right = refs[8:]
    count, side = 8, left.shape[0]
    share = side // count
    part = side // 4
    for k in range(count):
        other = lax.rem(ids[0] - k + count, count)
        start = pl.multiple_of(other * share, share)
        for j in range(3):
            lane = pl.multiple_of(lax.rem(other // 2 + j, 4) * part, part)
            here = slice(j * part, (j + 1) * part)
            left[pl.ds(start, share), pl.ds(lane, part)] = roots[k][0, :, here]
            right[pl.ds(start, share), pl.ds(lane, part)] = roots[k][1, :, here]
    for x in range(4):
        before = (x + 3) % 4
        at, to = slice(x * part, (x + 1) * part), slice(before * part, (before + 1) * part)
        left[at, to] = left[to, at].T
        right[at, to] = right[to, at].T
    lh[...], ll[...] = split(left[...])
    rh[...], rl[...] = split(right[...])


def apply_kernel(blocks, lh, ll, rh, rl, applied, gh, gl, whole):
    load_block(blocks, gh, gl)
    product = dot3((gh[...], gl[...]), (rh[...], rl[...]), ((1,), (0,)))
    value = dot3((lh[...], ll[...]), split(product), ((1,), (0,)))
    whole[...] = value
    norm = jnp.sqrt(jnp.sum(value * value, keepdims=True))
    scale = 1.0 / (norm + NORM_EPS)
    pieces, quarters, rows, _ = applied.shape
    for i in range(quarters):
        for r in range(pieces):
            at = (i * pieces + r) * rows
            applied[r, i] = whole[at : at + rows, :] * scale


def gram_kernel(ids, blocks, squares, *refs):
    outs = refs[:8]
    gh, gl, left, right = refs[8:]
    count, side = 8, left.shape[0]
    share = side // count
    load_block(blocks, gh, gl)
    g = (gh[...], gl[...])
    left[...] = dot3(g, g, ((1,), (1,)))
    right[...] = dot3(g, g, ((0,), (0,)))
    for k in range(count):
        start = pl.multiple_of(lax.rem(ids[0] + k, count) * share, share)
        outs[k][0:share, :] = left[pl.ds(start, share), :]
        outs[k][share : 2 * share, :] = right[pl.ds(start, share), :]
        outs[k][2 * share :, :] = squares[...]


def stat_kernel(ids, own, swapped, stat_left, stat_right, *refs):
    grams = refs[:8]
    moment_new, left, right = refs[8:]
    core = lax.rem(ids[0], 2)
    rows = own.shape[0] // 4
    for x in range(4):
        here = slice(x * rows, (x + 1) * rows)
        at = pl.multiple_of((2 * x + core) * rows, rows)
        moment_new[pl.ds(at, rows), :] = own[here, :]
        at = pl.multiple_of((2 * x + 1 - core) * rows, rows)
        moment_new[pl.ds(at, rows), :] = swapped[here, :]
    share = left.shape[1]
    for k in range(8):
        b = lax.rem(ids[0] - k + 8, 8)
        left[b] = SHAMPOO_DECAY * stat_left[b] + (1.0 - SHAMPOO_DECAY) * grams[k][0:share, :]
        right[b] = (
            SHAMPOO_DECAY * stat_right[b] + (1.0 - SHAMPOO_DECAY) * grams[k][share : 2 * share, :]
        )


def direction_kernel(ids, owner_cols, returned, direction):
    row = ids[1]
    width = returned.shape[-1]
    for o in range(returned.shape[0]):
        col = owner_cols[row, o]

        @pl.when(col >= 0)
        def _():
            start = pl.multiple_of(col * width, width)
            direction[:, pl.ds(start, width)] = returned[o]


def place_kernel(ids, *refs):
    pieces, grams, direction = refs[:8], refs[8:16], refs[16]
    held, tails, sems, out_sems = refs[17:]
    chip, core = ids[0] // 2, ids[0] % 2
    rows = pieces[0].shape[0]
    first, count = grams[0].shape[0] - 8, 8
    width = tails.shape[-1]
    loads = [
        pltpu.make_async_copy(gram.at[pl.ds(first, 8), :], tails.at[j], sems.at[j])
        for j, gram in enumerate(grams)
    ]
    loads = loads + [
        pltpu.make_async_copy(piece, held.at[j], sems.at[count + j])
        for j, piece in enumerate(pieces)
    ]
    for load in loads:
        load.start()
    for load in loads[:count]:
        load.wait()
    total = tails[0]
    for j in range(1, count):
        total = total + tails[j]
    norms = []
    for c in range(direction.shape[-1] // width):
        lane = (c // 8) * 128
        lanes = total[c % 8 : c % 8 + 1, lane : lane + 128]
        norms.append(jnp.sqrt(jnp.sum(lanes, axis=1, keepdims=True)))
    stores = []
    for j in range(count):
        loads[count + j].wait()
        for c, norm in enumerate(norms):
            here = slice(c * width, (c + 1) * width)
            held[j, :, here] = held[j, :, here] * norm
        owner = core if j < 4 else 1 - core
        start = pl.multiple_of((lax.rem(chip - j % 4 + 4, 4) * 2 + owner) * rows, rows)
        stores.append(
            pltpu.make_async_copy(held.at[j], direction.at[pl.ds(start, rows), :], out_sems.at[j])
        )
        stores[-1].start()
    for store in stores:
        store.wait()


def place(ids, pieces, grams, shape):
    hbm = pl.BlockSpec(memory_space=pltpu.HBM)
    ins = [*pieces, *grams]
    return pl.pallas_call(
        place_kernel,
        out_shape=pltpu.HBM(shape, F32),
        in_specs=[pl.BlockSpec(memory_space=pltpu.SMEM)] + [hbm] * len(ins),
        out_specs=hbm,
        scratch_shapes=[
            pltpu.VMEM((8, *pieces[0].shape), F32),
            pltpu.VMEM((8, 8, grams[0].shape[1]), F32),
            pltpu.SemaphoreType.DMA((16,)),
            pltpu.SemaphoreType.DMA((8,)),
        ],
        compiler_params=PARAMS,
    )(ids, *[pltpu.with_memory_space_constraint(x, pltpu.HBM) for x in ins])


def staged(kernel, cuts, n_small, n_in, n_out, *refs):
    cut = [n_small, n_in, n_out, n_in, n_out]
    groups, at = [], 0
    for size in cut:
        groups.append(refs[at : at + size])
        at += size
    small, sources, targets, ins, outs = groups
    sources = [
        src if cut is None else src.at[pl.ds(*cut), :] for src, cut in zip(sources, cuts)
    ]
    in_sems, out_sems = refs[at : at + 2]
    loads = [
        pltpu.make_async_copy(src, dst, in_sems.at[i])
        for i, (src, dst) in enumerate(zip(sources, ins))
    ]
    for load in loads:
        load.start()
    for load in loads:
        load.wait()
    kernel(*small, *ins, *outs, *refs[at + 2 :])
    stores = [
        pltpu.make_async_copy(src, dst, out_sems.at[i])
        for i, (src, dst) in enumerate(zip(outs, targets))
    ]
    for store in stores:
        store.start()
    for store in stores:
        store.wait()


def call(kernel, outs, small, ins, scratch, cuts=None, dtype=F32):
    hbm = pl.BlockSpec(memory_space=pltpu.HBM)
    smem = pl.BlockSpec(memory_space=pltpu.SMEM)
    cuts = cuts or [None] * len(ins)
    held = [
        pltpu.VMEM(x.shape if cut is None else (cut[1], *x.shape[1:]), x.dtype)
        for x, cut in zip(ins, cuts)
    ]
    held = held + [pltpu.VMEM(s, dtype) for s in outs]
    sems = [pltpu.SemaphoreType.DMA((len(ins),)), pltpu.SemaphoreType.DMA((len(outs),))]
    return pl.pallas_call(
        functools.partial(staged, kernel, cuts, len(small), len(ins), len(outs)),
        out_shape=[pltpu.HBM(shape, dtype) for shape in outs],
        in_specs=[smem] * len(small) + [hbm] * len(ins),
        out_specs=[hbm] * len(outs),
        scratch_shapes=held + sems + scratch,
        compiler_params=PARAMS,
    )(*small, *[pltpu.with_memory_space_constraint(x, pltpu.HBM) for x in ins])


def root_plan(ids, ins, outs):
    chip = ids[0] // 2
    for k, out in enumerate(outs):
        to = lax.rem(ids[0] + k, 8)
        for side in range(2):
            for j in range(3):
                lane = pl.multiple_of(lax.rem(chip + j, 4) * 128, 128)
                yield (
                    ins[side].at[to, :, pl.ds(lane, 128)],
                    out.at[side, :, slice(j * 128, (j + 1) * 128)],
                )


def copying(plan, split_stores, n_small, n_in, n_out, *refs):
    small, ins = refs[:n_small], refs[n_small : n_small + n_in]
    outs = refs[n_small + n_in : n_small + n_in + n_out]
    held, (sems, out_sems) = refs[n_small + n_in + n_out : -2], refs[-2:]
    loads = [
        pltpu.make_async_copy(src, dst, sems.at[i])
        for i, (src, dst) in enumerate(plan(*small, ins, held))
    ]
    pairs = zip(held, outs)
    if split_stores:
        landed = [dst for _, dst in plan(*small, ins, held)]
        pairs = zip(landed, [dst for _, dst in plan(*small, ins, outs)])
    stores = [
        pltpu.make_async_copy(src, dst, out_sems.at[i]) for i, (src, dst) in enumerate(pairs)
    ]
    for load in loads:
        load.start()
    for i, load in enumerate(loads):
        load.wait()
        if split_stores:
            stores[i].start()
    if not split_stores:
        for store in stores:
            store.start()
    for store in stores:
        store.wait()


def shuffle(plan, outs, small, ins, count, split_stores=False):
    hbm = pl.BlockSpec(memory_space=pltpu.HBM)
    smem = pl.BlockSpec(memory_space=pltpu.SMEM)
    return pl.pallas_call(
        functools.partial(copying, plan, split_stores, len(small), len(ins), len(outs)),
        out_shape=[pltpu.HBM(shape, F32) for shape in outs],
        in_specs=[smem] * len(small) + [hbm] * len(ins),
        out_specs=[hbm] * len(outs),
        scratch_shapes=[pltpu.VMEM(shape, F32) for shape in outs]
        + [pltpu.SemaphoreType.DMA((count,))] * 2,
        compiler_params=PARAMS,
    )(*small, *[pltpu.with_memory_space_constraint(x, pltpu.HBM) for x in ins])


def shards(gradient, second_moment, owner_cols, stat_left, stat_right, root_left, root_right):
    shard_rows, full_width = gradient.shape[1:]
    side = stat_left.shape[-1]
    owners = lax.axis_size("fsdp")
    reps = lax.axis_size("rep")
    chips = reps // 2
    cols = full_width // side
    rows = shard_rows // reps
    share = side // reps
    quarters = side // shard_rows
    block_rows = owner_cols.shape[0]
    rep = lax.axis_index("rep")
    chip, core = rep // 2, rep % 2
    my_row = lax.axis_index("fsdp") // quarters
    ids = jnp.stack([rep, my_row]).astype(jnp.int32)
    oc = owner_cols[:, 0, :]
    barrier = lax.optimization_barrier

    grad = gradient[0].reshape(chips, 2, rows, full_width)
    swap = [(i, i ^ 1) for i in range(reps)]
    other = lax.ppermute(pick(grad, 1 - core, 1), "rep", swap)
    mine = pick(grad, core, 1)
    parts = []
    for k in range(chips):
        to = (chip + k) % chips
        piece = pick(mine, to) + pick(other, to)
        parts.append(piece if k == 0 else rep_shift(piece, 2 * k, reps))
    second = lax.dynamic_slice_in_dim(second_moment, rep * rows, rows, 0)
    later_ids, _ = barrier((ids, parts[0]))
    stats = (block_rows, share, side)
    pair = (2, share, side)
    root_pair = (2, share, 3 * side // 4)
    roots = shuffle(
        root_plan,
        [root_pair] * reps,
        [later_ids],
        [root_left[0, 0], root_right[0, 0]],
        6 * reps,
    )
    ids, *roots = barrier((ids, *roots))

    strip = (rows, full_width)
    tail = (8, side)
    moment, squares, packed = call(
        functools.partial(moment_kernel, cols, reps),
        [strip, tail, (owners, rows, side)],
        [ids, oc],
        [*parts, second],
        [pltpu.VMEM(strip, F32)],
    )
    lines = [[2 * x + c for x in range(chips)] for c in range(2)]
    moment_line = lax.all_gather(moment, "rep", axis=0, tiled=True, axis_index_groups=lines)
    packed, *roots = barrier((packed, *roots))
    arrived = lax.all_to_all(packed, "fsdp", 0, 0, tiled=True)
    roots = [r if k == 0 else rep_shift(r, k, reps) for k, r in enumerate(roots)]
    arrived, squares, *roots = barrier((arrived, squares, *roots))

    square_sum = squares
    for bits in (1, 2, 3):
        square_sum = square_sum + lax.ppermute(
            squares, "fsdp", [(i, i ^ bits) for i in range(owners)]
        )
    blocks = lax.all_to_all(
        arrived.reshape(block_rows, quarters, rows, side), "rep", 0, 0, tiled=True
    )
    half = pltpu.VMEM((side, side), BF16)
    full = pltpu.VMEM((side, side), F32)
    halves = call(
        root_kernel, [(side, side)] * 4, [ids], roots, [full] * 2, dtype=BF16
    )
    (applied,) = call(
        apply_kernel, [blocks.shape], [], [blocks, *halves], [half] * 2 + [full]
    )
    spread = lax.all_to_all(applied, "rep", 0, 0, tiled=True)
    grams = call(
        gram_kernel,
        [(2 * share + 8, side)] * reps,
        [ids],
        [blocks, square_sum],
        [half] * 2 + [full] * 2,
    )
    spread, moment_line, *grams = barrier((spread, moment_line, *grams))
    moment_swap = lax.ppermute(moment_line, "rep", swap)
    returned = lax.all_to_all(spread.reshape(owners, rows, side), "fsdp", 0, 0, tiled=True)
    grams = [g if k == 0 else rep_shift(g, k, reps) for k, g in enumerate(grams)]
    returned, moment_swap = barrier((returned, moment_swap))
    (part,) = call(direction_kernel, [strip], [ids, oc], [returned], [])
    found = [part] + [rep_shift(part, 2 * k, reps) for k in range(1, chips)]
    last_ids, _ = barrier((ids, part))
    moment_new, left_new, right_new = call(
        stat_kernel,
        [(shard_rows, full_width), stats, stats],
        [last_ids],
        [moment_line, moment_swap, stat_left[0, 0], stat_right[0, 0], *grams],
        [],
    )
    found[2], left_new = barrier((found[2], left_new))
    swapped = [lax.ppermute(x, "rep", swap) for x in found]
    direction = place(ids, found + swapped, grams, (shard_rows, full_width))
    return (direction, moment_new, left_new[None, None], right_new[None, None])


def solution(mesh):
    return jax.shard_map(
        shards,
        mesh=mesh,
        in_specs=(
            P("rep", "fsdp", None),
            P("fsdp", None),
            P(),
            P("fsdp", None, None, "rep", None),
            P("fsdp", None, None, "rep", None),
            P("fsdp", None, None, "rep", None),
            P("fsdp", None, None, "rep", None),
        ),
        out_specs=(
            P("fsdp", None),
            P("fsdp", None),
            P("fsdp", None, None, "rep", None),
            P("fsdp", None, None, "rep", None),
        ),
        check_vma=False,
    )
```

```python
import functools

import jax
import jax.numpy as jnp
from jax import lax
from jax.experimental import pallas as pl
from jax.experimental.pallas import tpu as pltpu
from jax.sharding import PartitionSpec as P

SHAMPOO_DECAY = 0.9
ADAM_DECAY = 0.95
ADAM_EPS = 1e-08
NORM_EPS = 1e-06
PARAMS = pltpu.CompilerParams(vmem_limit_bytes=32 * 1024 * 1024)
F32 = jnp.float32
BF16 = jnp.bfloat16


def rep_shift(value, step, count):
    return lax.ppermute(value, "rep", [(i, (i + step) % count) for i in range(count)])


def pick(array, index, axis=0):
    return lax.dynamic_index_in_dim(array, index, axis, keepdims=False)


def split(value):
    high = value.astype(BF16)
    return high, (value - high.astype(F32)).astype(BF16)


def dot3(a, b, dims):
    dot = functools.partial(
        lax.dot_general, dimension_numbers=(dims, ((), ())), preferred_element_type=F32
    )
    return dot(a[0], b[0]) + (dot(a[0], b[1]) + dot(a[1], b[0]))


def moment_kernel(cols, replicas, ids, owner_cols, *refs):
    parts, second = refs[:4], refs[4]
    moment, squares, packed, averaged = refs[5:]
    row = ids[1]
    width = packed.shape[-1]
    squares[...] = jnp.zeros_like(squares)
    for c in range(cols):
        here = slice(c * width, (c + 1) * width)
        summed = (parts[0][:, here] + parts[1][:, here]) + (parts[2][:, here] + parts[3][:, here])
        mean = summed / replicas
        averaged[:, here] = mean
        new = ADAM_DECAY * second[:, here] + (1.0 - ADAM_DECAY) * mean * mean
        moment[:, here] = new
        step = mean / (jnp.sqrt(new) + ADAM_EPS)
        square = jnp.sum(step * step, axis=0, keepdims=True)
        lanes = square[:, 0:128]
        for k in range(1, width // 128):
            lanes = lanes + square[:, k * 128 : (k + 1) * 128]
        lane = (c // 8) * 128
        squares[c % 8 : c % 8 + 1, lane : lane + 128] = lanes
    for o in range(packed.shape[0]):
        col = owner_cols[row, o]
        start = pl.multiple_of(jnp.maximum(col, 0) * width, width)
        piece = averaged[:, pl.ds(start, width)]
        packed[o] = jnp.where(col >= 0, piece, 0.0)


def load_block(blocks, high, low):
    pieces, quarters, rows, _ = blocks.shape
    for i in range(quarters):
        for r in range(pieces):
            at = (i * pieces + r) * rows
            high[at : at + rows, :], low[at : at + rows, :] = split(blocks[r, i])


def root_kernel(ids, *refs):
    roots = refs[:8]
    lh, ll, rh, rl, left, right = refs[8:]
    count, side = 8, left.shape[0]
    share = side // count
    part = side // 4
    for k in range(count):
        other = lax.rem(ids[0] - k + count, count)
        start = pl.multiple_of(other * share, share)
        for j in range(3):
            lane = pl.multiple_of(lax.rem(other // 2 + j, 4) * part, part)
            here = slice(j * part, (j + 1) * part)
            left[pl.ds(start, share), pl.ds(lane, part)] = roots[k][0, :, here]
            right[pl.ds(start, share), pl.ds(lane, part)] = roots[k][1, :, here]
    for x in range(4):
        before = (x + 3) % 4
        at, to = slice(x * part, (x + 1) * part), slice(before * part, (before + 1) * part)
        left[at, to] = left[to, at].T
        right[at, to] = right[to, at].T
    lh[...], ll[...] = split(left[...])
    rh[...], rl[...] = split(right[...])


def apply_kernel(blocks, lh, ll, rh, rl, applied, gh, gl, whole):
    load_block(blocks, gh, gl)
    product = dot3((gh[...], gl[...]), (rh[...], rl[...]), ((1,), (0,)))
    value = dot3((lh[...], ll[...]), split(product), ((1,), (0,)))
    whole[...] = value
    norm = jnp.sqrt(jnp.sum(value * value, keepdims=True))
    scale = 1.0 / (norm + NORM_EPS)
    pieces, quarters, rows, _ = applied.shape
    for i in range(quarters):
        for r in range(pieces):
            at = (i * pieces + r) * rows
            applied[r, i] = whole[at : at + rows, :] * scale


def gram_kernel(ids, blocks, squares, *refs):
    outs = refs[:8]
    gh, gl, left, right = refs[8:]
    count, side = 8, left.shape[0]
    share = side // count
    load_block(blocks, gh, gl)
    g = (gh[...], gl[...])
    left[...] = dot3(g, g, ((1,), (1,)))
    right[...] = dot3(g, g, ((0,), (0,)))
    for k in range(count):
        start = pl.multiple_of(lax.rem(ids[0] + k, count) * share, share)
        outs[k][0:share, :] = left[pl.ds(start, share), :]
        outs[k][share : 2 * share, :] = right[pl.ds(start, share), :]
        outs[k][2 * share :, :] = squares[...]


def stat_kernel(ids, own, swapped, stat_left, stat_right, *refs):
    grams = refs[:8]
    moment_new, left, right = refs[8:]
    core = lax.rem(ids[0], 2)
    rows = own.shape[0] // 4
    for x in range(4):
        here = slice(x * rows, (x + 1) * rows)
        at = pl.multiple_of((2 * x + core) * rows, rows)
        moment_new[pl.ds(at, rows), :] = own[here, :]
        at = pl.multiple_of((2 * x + 1 - core) * rows, rows)
        moment_new[pl.ds(at, rows), :] = swapped[here, :]
    share = left.shape[1]
    for k in range(8):
        b = lax.rem(ids[0] - k + 8, 8)
        left[b] = SHAMPOO_DECAY * stat_left[b] + (1.0 - SHAMPOO_DECAY) * grams[k][0:share, :]
        right[b] = (
            SHAMPOO_DECAY * stat_right[b] + (1.0 - SHAMPOO_DECAY) * grams[k][share : 2 * share, :]
        )


def direction_kernel(ids, owner_cols, returned, *refs):
    grams = refs[:8]
    direction, norms = refs[8:]
    row = ids[1]
    width = returned.shape[-1]
    total = grams[0][...]
    for k in range(1, 8):
        total = total + grams[k][...]
    for c in range(direction.shape[-1] // width):
        lane = (c // 8) * 128
        lanes = total[c % 8 : c % 8 + 1, lane : lane + 128]
        norm = jnp.sqrt(jnp.sum(lanes, axis=1, keepdims=True))
        norms[c : c + 1, :] = jnp.broadcast_to(norm, (1, 128))
    for o in range(returned.shape[0]):
        col = owner_cols[row, o]

        @pl.when(col >= 0)
        def _():
            norm = norms[pl.ds(col, 1), :][:, 0:1]
            start = pl.multiple_of(col * width, width)
            direction[:, pl.ds(start, width)] = returned[o] * norm


def staged(kernel, cuts, n_small, n_in, n_out, *refs):
    cut = [n_small, n_in, n_out, n_in, n_out]
    groups, at = [], 0
    for size in cut:
        groups.append(refs[at : at + size])
        at += size
    small, sources, targets, ins, outs = groups
    sources = [
        src if cut is None else src.at[pl.ds(*cut), :] for src, cut in zip(sources, cuts)
    ]
    in_sems, out_sems = refs[at : at + 2]
    loads = [
        pltpu.make_async_copy(src, dst, in_sems.at[i])
        for i, (src, dst) in enumerate(zip(sources, ins))
    ]
    for load in loads:
        load.start()
    for load in loads:
        load.wait()
    kernel(*small, *ins, *outs, *refs[at + 2 :])
    stores = [
        pltpu.make_async_copy(src, dst, out_sems.at[i])
        for i, (src, dst) in enumerate(zip(outs, targets))
    ]
    for store in stores:
        store.start()
    for store in stores:
        store.wait()


def call(kernel, outs, small, ins, scratch, cuts=None, dtype=F32):
    hbm = pl.BlockSpec(memory_space=pltpu.HBM)
    smem = pl.BlockSpec(memory_space=pltpu.SMEM)
    cuts = cuts or [None] * len(ins)
    held = [
        pltpu.VMEM(x.shape if cut is None else (cut[1], *x.shape[1:]), x.dtype)
        for x, cut in zip(ins, cuts)
    ]
    held = held + [pltpu.VMEM(s, dtype) for s in outs]
    sems = [pltpu.SemaphoreType.DMA((len(ins),)), pltpu.SemaphoreType.DMA((len(outs),))]
    return pl.pallas_call(
        functools.partial(staged, kernel, cuts, len(small), len(ins), len(outs)),
        out_shape=[pltpu.HBM(shape, dtype) for shape in outs],
        in_specs=[smem] * len(small) + [hbm] * len(ins),
        out_specs=[hbm] * len(outs),
        scratch_shapes=held + sems + scratch,
        compiler_params=PARAMS,
    )(*small, *[pltpu.with_memory_space_constraint(x, pltpu.HBM) for x in ins])


def root_plan(ids, ins, outs):
    chip = ids[0] // 2
    for k, out in enumerate(outs):
        to = lax.rem(ids[0] + k, 8)
        for side in range(2):
            for j in range(3):
                lane = pl.multiple_of(lax.rem(chip + j, 4) * 128, 128)
                yield (
                    ins[side].at[to, :, pl.ds(lane, 128)],
                    out.at[side, :, slice(j * 128, (j + 1) * 128)],
                )


def place_plan(ids, ins, outs):
    chip, core = ids[0] // 2, ids[0] % 2
    rows = ins[0].shape[0]
    for j, piece in enumerate(ins):
        owner = core if j < 4 else 1 - core
        start = pl.multiple_of((lax.rem(chip - j % 4 + 4, 4) * 2 + owner) * rows, rows)
        yield piece, outs[0].at[pl.ds(start, rows), :]


def copying(plan, split_stores, n_small, n_in, n_out, *refs):
    small, ins = refs[:n_small], refs[n_small : n_small + n_in]
    outs = refs[n_small + n_in : n_small + n_in + n_out]
    held, (sems, out_sems) = refs[n_small + n_in + n_out : -2], refs[-2:]
    loads = [
        pltpu.make_async_copy(src, dst, sems.at[i])
        for i, (src, dst) in enumerate(plan(*small, ins, held))
    ]
    pairs = zip(held, outs)
    if split_stores:
        landed = [dst for _, dst in plan(*small, ins, held)]
        pairs = zip(landed, [dst for _, dst in plan(*small, ins, outs)])
    stores = [
        pltpu.make_async_copy(src, dst, out_sems.at[i]) for i, (src, dst) in enumerate(pairs)
    ]
    for load in loads:
        load.start()
    for i, load in enumerate(loads):
        load.wait()
        if split_stores:
            stores[i].start()
    if not split_stores:
        for store in stores:
            store.start()
    for store in stores:
        store.wait()


def shuffle(plan, outs, small, ins, count, split_stores=False):
    hbm = pl.BlockSpec(memory_space=pltpu.HBM)
    smem = pl.BlockSpec(memory_space=pltpu.SMEM)
    return pl.pallas_call(
        functools.partial(copying, plan, split_stores, len(small), len(ins), len(outs)),
        out_shape=[pltpu.HBM(shape, F32) for shape in outs],
        in_specs=[smem] * len(small) + [hbm] * len(ins),
        out_specs=[hbm] * len(outs),
        scratch_shapes=[pltpu.VMEM(shape, F32) for shape in outs]
        + [pltpu.SemaphoreType.DMA((count,))] * 2,
        compiler_params=PARAMS,
    )(*small, *[pltpu.with_memory_space_constraint(x, pltpu.HBM) for x in ins])


def shards(gradient, second_moment, owner_cols, stat_left, stat_right, root_left, root_right):
    shard_rows, full_width = gradient.shape[1:]
    side = stat_left.shape[-1]
    owners = lax.axis_size("fsdp")
    reps = lax.axis_size("rep")
    chips = reps // 2
    cols = full_width // side
    rows = shard_rows // reps
    share = side // reps
    quarters = side // shard_rows
    block_rows = owner_cols.shape[0]
    rep = lax.axis_index("rep")
    chip, core = rep // 2, rep % 2
    my_row = lax.axis_index("fsdp") // quarters
    ids = jnp.stack([rep, my_row]).astype(jnp.int32)
    oc = owner_cols[:, 0, :]
    barrier = lax.optimization_barrier

    grad = gradient[0].reshape(chips, 2, rows, full_width)
    swap = [(i, i ^ 1) for i in range(reps)]
    other = lax.ppermute(pick(grad, 1 - core, 1), "rep", swap)
    mine = pick(grad, core, 1)
    parts = []
    for k in range(chips):
        to = (chip + k) % chips
        piece = pick(mine, to) + pick(other, to)
        parts.append(piece if k == 0 else rep_shift(piece, 2 * k, reps))
    second = lax.dynamic_slice_in_dim(second_moment, rep * rows, rows, 0)
    later_ids, _ = barrier((ids, parts[0]))
    stats = (block_rows, share, side)
    pair = (2, share, side)
    root_pair = (2, share, 3 * side // 4)
    roots = shuffle(
        root_plan,
        [root_pair] * reps,
        [later_ids],
        [root_left[0, 0], root_right[0, 0]],
        6 * reps,
    )
    ids, *roots = barrier((ids, *roots))

    strip = (rows, full_width)
    tail = (8, side)
    moment, squares, packed = call(
        functools.partial(moment_kernel, cols, reps),
        [strip, tail, (owners, rows, side)],
        [ids, oc],
        [*parts, second],
        [pltpu.VMEM(strip, F32)],
    )
    lines = [[2 * x + c for x in range(chips)] for c in range(2)]
    moment_line = lax.all_gather(moment, "rep", axis=0, tiled=True, axis_index_groups=lines)
    packed, *roots = barrier((packed, *roots))
    arrived = lax.all_to_all(packed, "fsdp", 0, 0, tiled=True)
    roots = [r if k == 0 else rep_shift(r, k, reps) for k, r in enumerate(roots)]
    arrived, squares, *roots = barrier((arrived, squares, *roots))

    square_sum = squares
    for bits in (1, 2, 3):
        square_sum = square_sum + lax.ppermute(
            squares, "fsdp", [(i, i ^ bits) for i in range(owners)]
        )
    blocks = lax.all_to_all(
        arrived.reshape(block_rows, quarters, rows, side), "rep", 0, 0, tiled=True
    )
    half = pltpu.VMEM((side, side), BF16)
    full = pltpu.VMEM((side, side), F32)
    halves = call(
        root_kernel, [(side, side)] * 4, [ids], roots, [full] * 2, dtype=BF16
    )
    (applied,) = call(
        apply_kernel, [blocks.shape], [], [blocks, *halves], [half] * 2 + [full]
    )
    spread = lax.all_to_all(applied, "rep", 0, 0, tiled=True)
    grams = call(
        gram_kernel,
        [(2 * share + 8, side)] * reps,
        [ids],
        [blocks, square_sum],
        [half] * 2 + [full] * 2,
    )
    spread, moment_line, *grams = barrier((spread, moment_line, *grams))
    moment_swap = lax.ppermute(moment_line, "rep", swap)
    returned = lax.all_to_all(spread.reshape(owners, rows, side), "fsdp", 0, 0, tiled=True)
    grams = [g if k == 0 else rep_shift(g, k, reps) for k, g in enumerate(grams)]
    returned, *grams = barrier((returned, *grams))
    tails = (2 * share, 8)
    (part,) = call(
        direction_kernel,
        [strip],
        [ids, oc],
        [returned, *grams],
        [pltpu.VMEM((16, 128), F32)],
        [None] + [tails] * reps,
    )
    found = [part] + [rep_shift(part, 2 * k, reps) for k in range(1, chips)]
    last_ids, _ = barrier((ids, part))
    moment_new, left_new, right_new = call(
        stat_kernel,
        [(shard_rows, full_width), stats, stats],
        [last_ids],
        [moment_line, moment_swap, stat_left[0, 0], stat_right[0, 0], *grams],
        [],
    )
    found[2], left_new = barrier((found[2], left_new))
    swapped = [lax.ppermute(x, "rep", swap) for x in found]
    (direction,) = shuffle(
        place_plan,
        [(shard_rows, full_width)],
        [ids],
        found + swapped,
        2 * chips,
        True,
    )
    return (direction, moment_new, left_new[None, None], right_new[None, None])


def solution(mesh):
    return jax.shard_map(
        shards,
        mesh=mesh,
        in_specs=(
            P("rep", "fsdp", None),
            P("fsdp", None),
            P(),
            P("fsdp", None, None, "rep", None),
            P("fsdp", None, None, "rep", None),
            P("fsdp", None, None, "rep", None),
            P("fsdp", None, None, "rep", None),
        ),
        out_specs=(
            P("fsdp", None),
            P("fsdp", None),
            P("fsdp", None, None, "rep", None),
            P("fsdp", None, None, "rep", None),
        ),
        check_vma=False,
    )
```
